256 devices in a mesh: seq: 64 (over y_lo, x, z), head: 4 (over y_hi, core).
Axes of the slice: x: 4, y: 4 (y_hi: 2, y_lo: 2; y = y_hi * 2 + y_lo), z: 8, core: 2. Of those that a mesh axis runs over, the one named last changes fastest.
Arguments:
- queries: bfloat16 [8192, 1536], P('seq', 'head'), may hold values from -45 to 45
- keys: bfloat16 [8192, 1536], P('seq', 'head'), may hold values from -4 to 4
- values: bfloat16 [8192, 1536], P('seq', 'head'), may hold values from -6 to 6
- grad_y: bfloat16 [8192, 1536], P('seq', 'head'), may hold values from -384 to 384
- out_weight: bfloat16 [768, 768], P('head'), may hold values from -0.21875 to 0.21875
- counts: int32 [64], replicated, may hold values from 64 to 256, as said below
- offsets: int32 [2, 16], replicated, may hold values from 0 to 15, as said below
Outputs:
- grad_queries: bfloat16 [8192, 1536], P('seq', 'head')
- grad_keys: bfloat16 [8192, 1536], P('seq', 'head')
- grad_values: bfloat16 [8192, 1536], P('seq', 'head')
The draws below stay inside these ranges and needn't reach their ends.
Inputs may be any that keep to these rules, and one draw needn't show every extreme that they name: The first counts[s] rows of sequence shard s hold tissue, the rest are empty; some shard is full. `offsets`: row 0 lies below 4, row 1 below 16.
All inputs are finite; a program needn't handle non-finite values.
Results may differ from the reference program's by a relative error of at most 0.006.
Values may be sent and summed in bfloat16 or wider, within the bound.
No kernel may reach another device: no remote copies, remote signals or barrier semaphores. Data moves between devices by JAX's collectives and lax.ppermute only.
A program may use at most 64 MiB of HBM per device.

```python
import jax
import jax.numpy as jnp
from jax import lax

HEAD_TOTAL = 16
HEAD_SIZE = 48
D = 768
SHARD_TOKENS = 256
TOKEN_TOTAL = 16384
MIDDLE_SHARDS = 8
MIDDLE_DILATION = 4
TOP_DILATION = 16
N_SEQ = 64


def pair_layout(flat):
    return flat.reshape(TOKEN_TOTAL // 2, 2, HEAD_TOTAL, HEAD_SIZE).transpose(0, 2, 1, 3).reshape(TOKEN_TOTAL // 2, 2 * D)


def draw_queries(key, part):
    key = jax.random.fold_in(key, 1)
    sampled_rows = jax.random.truncated_normal(key, -4.0, 4.0, (TOKEN_TOTAL, D), jnp.float32)
    return pair_layout(sampled_rows).astype(jnp.bfloat16)


def draw_keys(key, part):
    key = jax.random.fold_in(key, 2)
    sampled_rows = jax.random.truncated_normal(key, -4.0, 4.0, (TOKEN_TOTAL, D), jnp.float32)
    return pair_layout(sampled_rows).astype(jnp.bfloat16)


def draw_counts(key, part):
    key = jax.random.fold_in(key, 3)
    lowest = SHARD_TOKENS // 4
    sampled_rows = jax.random.randint(key, (N_SEQ,), lowest, SHARD_TOKENS + 1)
    chosen_rows = jax.random.permutation(jax.random.fold_in(key, 7), N_SEQ)
    sampled_rows = sampled_rows.at[chosen_rows[0]].set(SHARD_TOKENS)
    sampled_rows = sampled_rows.at[chosen_rows[1]].set(lowest)
    return sampled_rows.astype(jnp.int32)


def draw_offsets(key, part):
    key = jax.random.fold_in(key, 4)
    raw_values = jax.random.randint(key, (2, HEAD_TOTAL), 0, 1 << 20)
    bounds_list = jnp.array([MIDDLE_DILATION, TOP_DILATION], jnp.int32)[:, None]
    sampled_rows = raw_values % bounds_list
    chosen_rows = jax.random.permutation(jax.random.fold_in(key, 9), HEAD_TOTAL)
    sampled_rows = sampled_rows.at[1, chosen_rows[0]].set(TOP_DILATION - 1)
    sampled_rows = sampled_rows.at[1, chosen_rows[1]].set(0)
    return sampled_rows.astype(jnp.int32)


def level_of(rng, extent, pieces, low, largest):
    level = 1.0
    for axis_at, parts in pieces:
        draws = jax.random.uniform(jax.random.fold_in(jax.random.fold_in(rng, 6), axis_at), (parts,), jnp.float32, low / len(pieces), largest / len(pieces))
        level = level * jnp.repeat(jnp.exp(draws), extent[axis_at] // parts).reshape((-1,) + (1,) * (len(extent) - 1 - axis_at))
    return level


def normal_values(own_key, dims, deviation, most, pieces=(), kind=jnp.bfloat16):
    entries = deviation * jax.random.normal(own_key, dims, jnp.float32)
    if pieces:
        entries = entries * level_of(own_key, dims, pieces, -0.22, 0.18)
    return jnp.clip(entries, -most, most).astype(kind)


def setup_inputs(seed: int = 0) -> dict:
    arg_keys = jax.random.split(jax.random.key(seed), 8)
    queries = draw_queries(jax.random.fold_in(arg_keys[7], 71), 0)
    keys = draw_keys(jax.random.fold_in(arg_keys[7], 71), 0)
    values = normal_values(arg_keys[2], (TOKEN_TOTAL // 2, 2 * D), 1.0, 6.0, ((0, 64), (1, 4)))
    grad_y = normal_values(arg_keys[3], (TOKEN_TOTAL // 2, 2 * D), 64.0, 384.0, ((0, 64), (1, 4)))
    out_weight = normal_values(arg_keys[4], (D, D), D ** -0.5, 0.21875, ((0, 4),))
    counts = draw_counts(jax.random.fold_in(arg_keys[7], 71), 0)
    offsets = draw_offsets(jax.random.fold_in(arg_keys[7], 71), 0)
    return {"queries": queries, "keys": keys, "values": values, "grad_y": grad_y, "out_weight": out_weight, "counts": counts, "offsets": offsets}


def to_tokens(paired):
    half_rows, width = paired.shape
    head_tally = width // (2 * HEAD_SIZE)
    return paired.reshape(half_rows, head_tally, 2, HEAD_SIZE).transpose(0, 2, 1, 3).reshape(2 * half_rows, head_tally * HEAD_SIZE)


def to_pairs(flat):
    row_tally, width = flat.shape
    head_tally = width // HEAD_SIZE
    return flat.reshape(row_tally // 2, 2, head_tally, HEAD_SIZE).transpose(0, 2, 1, 3).reshape(row_tally // 2, 2 * width)


def rounded(source_shard):
    return lax.optimization_barrier(source_shard.astype(jnp.bfloat16)).astype(jnp.float32)


def choose_rows(source_shard, dilation_rate, head_shifts):
    sparse_rows = source_shard.shape[0] // dilation_rate
    reshaped_rows = source_shard.reshape((sparse_rows, dilation_rate) + source_shard.shape[1:])
    pattern = jnp.arange(dilation_rate)[:, None] == head_shifts[None, :]
    pattern = pattern.reshape((1, dilation_rate, head_shifts.shape[0]) + (1,) * (source_shard.ndim - 2))
    return jnp.sum(jnp.where(pattern, reshaped_rows, jnp.zeros((), source_shard.dtype)), axis=1)


def position_rows(compress_rows, dilation_rate, head_shifts, filler):
    sparse_rows = compress_rows.shape[0]
    pattern = jnp.arange(dilation_rate)[:, None] == head_shifts[None, :]
    pattern = pattern.reshape((1, dilation_rate, head_shifts.shape[0]) + (1,) * (compress_rows.ndim - 2))
    expand_rows = jnp.where(pattern, compress_rows[:, None], jnp.asarray(filler, compress_rows.dtype))
    return expand_rows.reshape((sparse_rows * dilation_rate,) + compress_rows.shape[1:])


def rows_to_blocks(source_shard, segment_length):
    heads_leading = jnp.swapaxes(source_shard, 0, 1)
    return heads_leading.reshape((heads_leading.shape[0] * (heads_leading.shape[1] // segment_length), segment_length) + heads_leading.shape[2:])


def blocks_to_rows(source_shard, sparse_rows):
    heads_leading = source_shard.reshape((HEAD_TOTAL, sparse_rows) + source_shard.shape[2:])
    return jnp.swapaxes(heads_leading, 0, 1)


def forward_per_block(operands):
    query_tile_block, key_block, value_block, valid_keys = operands
    logit_scores = jnp.dot(query_tile_block, key_block.T, precision=lax.Precision.HIGHEST) * HEAD_SIZE ** -0.5
    logit_scores = jnp.where(valid_keys[None, :], logit_scores, -jnp.inf)
    row_maximum = jnp.max(logit_scores, axis=1)
    expo_vals = jnp.exp(logit_scores - row_maximum[:, None])
    exponent_sum = jnp.sum(expo_vals, axis=1)
    level_output = jnp.dot(rounded(expo_vals), value_block, precision=lax.Precision.HIGHEST)
    return row_maximum, exponent_sum, level_output


def backward_per_block(operands):
    query_tile_block, key_block, value_block, valid_keys, log_block, block_gradient, dot_block = operands
    score_scale = HEAD_SIZE ** -0.5
    logit_scores = jnp.dot(query_tile_block, key_block.T, precision=lax.Precision.HIGHEST) * score_scale
    attention_weight = jnp.where(valid_keys[None, :], jnp.exp(logit_scores - log_block[:, None]), 0.0)
    weight_rounded = rounded(attention_weight)
    value_gradient = jnp.dot(weight_rounded.T, block_gradient, precision=lax.Precision.HIGHEST)
    weight_gradient = jnp.dot(block_gradient, value_block.T, precision=lax.Precision.HIGHEST)
    grad_score = rounded(attention_weight * (weight_gradient - dot_block[:, None]))
    query_gradient = jnp.dot(grad_score, key_block, precision=lax.Precision.HIGHEST) * score_scale
    key_gradient = jnp.dot(grad_score.T, query_tile_block, precision=lax.Precision.HIGHEST) * score_scale
    return query_gradient, key_gradient, value_gradient


def reference(queries, keys, values, grad_y, out_weight, counts, offsets):
    query_lines = to_tokens(queries).astype(jnp.float32).reshape(TOKEN_TOTAL, HEAD_TOTAL, HEAD_SIZE)
    key_lines = to_tokens(keys).astype(jnp.float32).reshape(TOKEN_TOTAL, HEAD_TOTAL, HEAD_SIZE)
    value_lines = to_tokens(values).astype(jnp.float32).reshape(TOKEN_TOTAL, HEAD_TOTAL, HEAD_SIZE)
    position = jnp.arange(TOKEN_TOTAL)
    tissue = (position % SHARD_TOKENS) < counts[position // SHARD_TOKENS]
    zero_shifts = jnp.zeros((HEAD_TOTAL,), jnp.int32)
    level_list = ((1, 2 * SHARD_TOKENS, zero_shifts), (MIDDLE_DILATION, MIDDLE_SHARDS * SHARD_TOKENS, offsets[0]), (TOP_DILATION, TOKEN_TOTAL, offsets[1]))
    level_inputs = []
    row_maxima, exponent_sums, level_outputs = [], [], []
    for dilation_rate, segment, head_shifts in level_list:
        segment_length = segment // dilation_rate
        sparse_rows = TOKEN_TOTAL // dilation_rate
        chosen_positions = (jnp.arange(sparse_rows)[:, None] * dilation_rate + head_shifts[None, :]).astype(jnp.int32)
        valid_keys = tissue[chosen_positions]
        sparse_query = choose_rows(query_lines, dilation_rate, head_shifts)
        sparse_key = choose_rows(key_lines, dilation_rate, head_shifts)
        sparse_value = choose_rows(value_lines, dilation_rate, head_shifts)
        level_inputs.append((dilation_rate, segment_length, sparse_rows, head_shifts, sparse_query, sparse_key, sparse_value, valid_keys))
        row_maximum, exponent_sum, level_output = lax.map(forward_per_block, (rows_to_blocks(sparse_query, segment_length), rows_to_blocks(sparse_key, segment_length), rows_to_blocks(sparse_value, segment_length), rows_to_blocks(valid_keys, segment_length)))
        row_maxima.append(position_rows(blocks_to_rows(row_maximum, sparse_rows), dilation_rate, head_shifts, -jnp.inf))
        exponent_sums.append(position_rows(blocks_to_rows(exponent_sum, sparse_rows), dilation_rate, head_shifts, 0.0))
        level_outputs.append(position_rows(blocks_to_rows(level_output, sparse_rows), dilation_rate, head_shifts, 0.0))
    greatest = jnp.maximum(jnp.maximum(row_maxima[0], row_maxima[1]), row_maxima[2])
    scales = [jnp.exp(row_maximum - greatest) for row_maximum in row_maxima]
    norm_sum = exponent_sums[0] * scales[0] + exponent_sums[1] * scales[1] + exponent_sums[2] * scales[2]
    attended = (level_outputs[0] * scales[0][..., None] + level_outputs[1] * scales[1][..., None] + level_outputs[2] * scales[2][..., None]) / norm_sum[..., None]
    logsum_total = greatest + jnp.log(norm_sum)
    attend_grad = jnp.dot(to_tokens(grad_y), out_weight.T, preferred_element_type=jnp.float32)
    row_gradient = attend_grad.astype(jnp.bfloat16) * tissue[:, None].astype(jnp.bfloat16)
    row_gradient = row_gradient.astype(jnp.float32).reshape(TOKEN_TOTAL, HEAD_TOTAL, HEAD_SIZE)
    product_gradient = jnp.sum(row_gradient * attended, axis=-1)
    query_gradient = jnp.zeros((TOKEN_TOTAL, HEAD_TOTAL, HEAD_SIZE), jnp.float32)
    key_gradient = jnp.zeros((TOKEN_TOTAL, HEAD_TOTAL, HEAD_SIZE), jnp.float32)
    value_gradient = jnp.zeros((TOKEN_TOTAL, HEAD_TOTAL, HEAD_SIZE), jnp.float32)
    for dilation_rate, segment_length, sparse_rows, head_shifts, sparse_query, sparse_key, sparse_value, valid_keys in level_inputs:
        sparse_logsum = choose_rows(logsum_total, dilation_rate, head_shifts)
        sparse_gradient = choose_rows(row_gradient, dilation_rate, head_shifts)
        sparse_product = choose_rows(product_gradient, dilation_rate, head_shifts)
        piece_query, piece_key, piece_value = lax.map(backward_per_block, (rows_to_blocks(sparse_query, segment_length), rows_to_blocks(sparse_key, segment_length), rows_to_blocks(sparse_value, segment_length), rows_to_blocks(valid_keys, segment_length), rows_to_blocks(sparse_logsum, segment_length), rows_to_blocks(sparse_gradient, segment_length), rows_to_blocks(sparse_product, segment_length)))
        query_gradient = query_gradient + position_rows(blocks_to_rows(piece_query, sparse_rows), dilation_rate, head_shifts, 0.0)
        key_gradient = key_gradient + position_rows(blocks_to_rows(piece_key, sparse_rows), dilation_rate, head_shifts, 0.0)
        value_gradient = value_gradient + position_rows(blocks_to_rows(piece_value, sparse_rows), dilation_rate, head_shifts, 0.0)
    return (to_pairs(query_gradient.reshape(TOKEN_TOTAL, D).astype(jnp.bfloat16)), to_pairs(key_gradient.reshape(TOKEN_TOTAL, D).astype(jnp.bfloat16)), to_pairs(value_gradient.reshape(TOKEN_TOTAL, D).astype(jnp.bfloat16)))
```

```python
import math

import jax
import jax.numpy as jnp
from jax import lax
from jax.experimental import pallas as pl
from jax.experimental.pallas import tpu as pltpu
from jax.sharding import PartitionSpec as P

HEAD = 48
HEADS = 4
TOKENS = 256
HALF = TOKENS // 2
FEAT = HEADS * HEAD
LANES = 256
MID = 4
TOP = 16
GROUP = 8
ROWS1 = TOKENS // MID
ROWS2 = TOKENS // TOP
SCALE = HEAD**-0.5
ROOT = math.sqrt(HEAD)
EXP2 = SCALE * math.log2(math.e)
BIG = 1e30
BF = jnp.bfloat16
F32 = jnp.float32

VMEM = pl.BlockSpec(memory_space=pltpu.VMEM)
SMEM = pl.BlockSpec(memory_space=pltpu.SMEM)


def iota(shape, dim):
    return lax.broadcasted_iota(jnp.int32, shape, dim)


def nt(a, b):
    return lax.dot_general(a, b, (((1,), (1,)), ((), ())), preferred_element_type=F32)


def nn(a, b):
    return jnp.dot(a, b, preferred_element_type=F32)


def head_mask(h, shape):
    lane = iota(shape, 1)
    return ((lane >= HEAD * h) & (lane < HEAD * (h + 1))) | ((lane >= FEAT + 8 * h) & (lane < FEAT + 8 * h + 8))


def helper_lane(shape):
    lane = iota(shape, 1)
    return jnp.where((lane >= FEAT) & (lane < FEAT + 8 * HEADS), (lane - FEAT) & 7, 8)


def pair_matrix():
    row = iota((2 * FEAT, 2 * LANES), 0)
    col = iota((2 * FEAT, 2 * LANES), 1)
    parity = (col >= LANES).astype(jnp.int32)
    at = col - LANES * parity
    h = (at >= HEAD).astype(jnp.int32) + (at >= 2 * HEAD).astype(jnp.int32) + (at >= 3 * HEAD).astype(jnp.int32)
    hit = (row == at + HEAD * (h + parity)) & (at < FEAT)
    return jnp.where(hit, 1.0, 0.0).astype(BF)


def unpair_matrix():
    row = iota((2 * LANES, 2 * FEAT), 0)
    col = iota((2 * LANES, 2 * FEAT), 1)
    parity = (row >= LANES).astype(jnp.int32)
    at = row - LANES * parity
    h = (at >= HEAD).astype(jnp.int32) + (at >= 2 * HEAD).astype(jnp.int32) + (at >= 3 * HEAD).astype(jnp.int32)
    hit = (col == at + HEAD * (h + parity)) & (at < FEAT)
    return jnp.where(hit, 1.0, 0.0).astype(BF)


def by_parity(paired, matrix):
    both = nn(paired, matrix)
    return jnp.concatenate([both[:, :LANES], both[:, LANES:]], axis=0)


def to_paired(flat, matrix):
    wide = jnp.concatenate([flat[:HALF], flat[HALF:]], axis=1)
    return nn(wide, matrix).astype(BF)


def chosen(offsets, level, h, shape, dim):
    rate = MID if level == 0 else TOP
    place = rate * iota(shape, dim) + offsets[level, h]
    return ((place >> 1) + (place & 1) * HALF) == iota(shape, 1 - dim)


def select_stack(offsets, level):
    rows = ROWS1 if level == 0 else ROWS2
    return jnp.concatenate(
        [jnp.where(chosen(offsets, level, h, (rows, TOKENS), 0), 1.0, 0.0) for h in range(HEADS)], axis=0
    ).astype(BF)


def masked_stack(stack, rows):
    return jnp.concatenate(
        [jnp.where(head_mask(h, (rows, LANES)), stack[h * rows : (h + 1) * rows], 0.0) for h in range(HEADS)], axis=0
    )


def folded(stack, rows):
    total = stack[:rows]
    for h in range(1, HEADS):
        total = total + stack[h * rows : (h + 1) * rows]
    return total


def split3(x):
    high = x.astype(BF)
    rest = x - high.astype(F32)
    mid = rest.astype(BF)
    low = (rest - mid.astype(F32)).astype(BF)
    return high, mid, low


def prep_kernel(offsets, count, q, k, v, qt, kt, vt, s1, s2):
    matrix = pair_matrix()
    tile = (TOKENS, LANES)
    row = iota(tile, 0)
    place = jnp.where(row < HALF, 2 * row, 2 * (row - HALF) + 1)
    helper = helper_lane(tile)
    key_mask = jnp.where(place < count[0], 0.0, -BIG)
    q_aux = jnp.where(helper == 3, 1.0, 0.0)
    k_aux = jnp.where(helper < 3, -1.0, jnp.where(helper == 3, key_mask, 0.0))
    v_aux = jnp.where((helper >= 4) & (helper < 7), -1.0, 0.0)
    first = select_stack(offsets, 0)
    second = select_stack(offsets, 1)
    for n, (src, aux, dst) in enumerate(((q, q_aux, qt), (k, k_aux, kt), (v, v_aux, vt))):
        flat = (by_parity(src[...], matrix) + aux).astype(BF)
        dst[...] = flat
        cols = slice(n * LANES, (n + 1) * LANES)
        s1[:, cols] = folded(masked_stack(nn(first, flat), ROWS1), ROWS1).astype(BF)
        s2[:, cols] = folded(masked_stack(nn(second, flat), ROWS2), ROWS2).astype(BF)


def proj_kernel(count, gy, w, g):
    matrix = pair_matrix()
    total = jnp.zeros((TOKENS, FEAT), F32)
    for i in range(4):
        flat = by_parity(gy[i], matrix).astype(BF)
        total = total + nt(flat[:, :FEAT], w[:, i * FEAT : (i + 1) * FEAT])
    row = iota((TOKENS, FEAT), 0)
    place = jnp.where(row < HALF, 2 * row, 2 * (row - HALF) + 1)
    total = jnp.where(place < count[0], total, 0.0)
    g[...] = jnp.concatenate([total, jnp.zeros((TOKENS, LANES - FEAT), F32)], axis=1).astype(BF)


def level_stats(key_parts, value_parts, queries, grads):
    scores = [nt(k, queries) for k in key_parts]
    top = scores[0].max(axis=0, keepdims=True)
    for s in scores[1:]:
        top = jnp.maximum(top, s.max(axis=0, keepdims=True))
    mass = dot = None
    for s, v in zip(scores, value_parts):
        e = jnp.exp2((s - top) * EXP2)
        part = e.sum(axis=0, keepdims=True)
        part_dot = (e * nt(v, grads)).sum(axis=0, keepdims=True)
        mass = part if mass is None else mass + part
        dot = part_dot if dot is None else dot + part_dot
    return top, mass, dot


def spread(stats, stack, rows):
    top, mass, dot = stats
    width = top.shape[1]
    lane = iota((HEADS, width), 1)
    own = (lane >= rows * iota((HEADS, width), 0)) & (lane < rows * (iota((HEADS, width), 0) + 1))
    placed = [jnp.where(own, x, 0.0) for x in (top, mass, dot, jnp.ones_like(top))]
    placed = jnp.concatenate(placed, axis=0)
    out = sum(nn(term, stack) for term in split3(placed))
    there = out[12:16] > 0.5
    return jnp.where(there, out[0:4], -BIG), out[4:8], out[8:12]


def forward_kernel(offsets, q, g, k, v, kp, vp, kv1, kv2, gt, g1, g2):
    first = select_stack(offsets, 0)
    second = jnp.concatenate([select_stack(offsets, 1), jnp.zeros((128 - HEADS * ROWS2, TOKENS), BF)], axis=0)
    queries, grads = q[...], g[...]
    tops, masses, dots = [], [], []
    for h in range(HEADS):
        mask = head_mask(h, (1, LANES)).astype(BF)
        top, mass, dot = level_stats((k[...], kp[...]), (v[...], vp[...]), queries * mask, grads * mask)
        tops.append(top)
        masses.append(mass)
        dots.append(dot)
    top0, mass0, dot0 = (jnp.concatenate(x, axis=0) for x in (tops, masses, dots))

    def stack_of(select, x, rows):
        full = nn(select, x)
        parts = [masked_stack(full[: HEADS * rows], rows)]
        if full.shape[0] > HEADS * rows:
            parts.append(full[HEADS * rows :])
        return jnp.concatenate(parts, axis=0).astype(BF)

    stats1 = level_stats(
        (kv1[:, :LANES],), (kv1[:, LANES:],), stack_of(first, queries, ROWS1), stack_of(first, grads, ROWS1)
    )
    stats2 = level_stats(
        (kv2[:, :LANES],), (kv2[:, LANES:],), stack_of(second, queries, ROWS2), stack_of(second, grads, ROWS2)
    )
    top1, mass1, dot1 = spread(stats1, first, ROWS1)
    top2, mass2, dot2 = spread(stats2, second, ROWS2)
    top = jnp.maximum(jnp.maximum(top0, top1), top2)
    f0, f1, f2 = (jnp.exp2((x - top) * EXP2) for x in (top0, top1, top2))
    total = mass0 * f0 + mass1 * f1 + mass2 * f2
    grad_dot = (dot0 * f0 + dot1 * f1 + dot2 * f2) / total
    log_total = top + jnp.log(total) * ROOT
    rows = jnp.concatenate(
        [x.astype(F32) for x in (*split3(log_total), *split3(grad_dot))]
        + [jnp.ones((HEADS, TOKENS), F32), jnp.zeros((HEADS, TOKENS), F32)],
        axis=0,
    )
    at = iota((8 * HEADS, LANES), 0)
    s, h = at >> 2, at & 3
    slot = jnp.where(s < 3, s, jnp.where(s < 6, s + 1, jnp.where(s == 6, 3, 7)))
    place = jnp.where(iota((8 * HEADS, LANES), 1) == FEAT + 8 * h + slot, 1.0, 0.0).astype(BF)
    full = grads.astype(F32) + nn(rows.T.astype(BF), place)
    full = full.astype(BF)
    gt[...] = full
    g1[...] = folded(masked_stack(nn(first, full), ROWS1), ROWS1).astype(BF)
    g2[...] = folded(masked_stack(nn(second, full)[: HEADS * ROWS2], ROWS2), ROWS2).astype(BF)


def with_helpers(x, helpers):
    return jnp.where(iota(x.shape, 1) < FEAT, x, helpers)


def feature_mask(h, shape):
    lane = iota(shape, 1)
    return (lane >= HEAD * h) & (lane < HEAD * (h + 1))


def scatter_rows(offsets, parts1, parts2):
    total = None
    for level, part, rows in ((0, parts1, ROWS1), (1, parts2, ROWS2)):
        place = jnp.concatenate(
            [jnp.where(chosen(offsets, level, h, (TOKENS, rows), 1), 1.0, 0.0) for h in range(HEADS)], axis=1
        ).astype(BF)
        part = jnp.concatenate(
            [jnp.where(feature_mask(h, (rows, LANES)), part[h * rows : (h + 1) * rows], 0.0) for h in range(HEADS)],
            axis=0,
        )
        high = part.astype(BF)
        low = (part - high.astype(F32)).astype(BF)
        got = nn(place, high) + nn(place, low)
        total = got if total is None else total + got
    return total


def grad_query_kernel(offsets, q, gt, k, v, kp, vp, kv1, kv2, dq):
    first, second = select_stack(offsets, 0), select_stack(offsets, 1)
    grads = gt[...]
    queries = with_helpers(q[...], grads)

    def back(queries, grads, keys, values):
        total = None
        for kk, vv in zip(keys, values):
            weight = jnp.exp2(nt(queries, kk) * EXP2)
            score = (weight * nt(grads, vv)).astype(BF)
            part = nn(score, kk)
            total = part if total is None else total + part
        return total

    total = jnp.zeros((TOKENS, LANES), F32)
    for h in range(HEADS):
        mask = head_mask(h, (1, LANES)).astype(BF)
        part = back(queries * mask, grads * mask, (k[...], kp[...]), (v[...], vp[...]))
        total = jnp.where(feature_mask(h, (TOKENS, LANES)), part, total)
    q1 = masked_stack(nn(first, queries), ROWS1).astype(BF)
    g1 = masked_stack(nn(first, grads), ROWS1).astype(BF)
    q2 = masked_stack(nn(second, queries), ROWS2).astype(BF)
    g2 = masked_stack(nn(second, grads), ROWS2).astype(BF)
    part1 = back(q1, g1, (kv1[:, :LANES],), (kv1[:, LANES:],))
    part2 = back(q2, g2, (kv2[:, :LANES],), (kv2[:, LANES:],))
    total = (total + scatter_rows(offsets, part1, part2)) * SCALE
    dq[...] = to_paired(total.astype(BF), unpair_matrix())


def grad_key_kernel(offsets, k, v, q, gt, qp, gp, q1, g1, q2, g2, dk, dv):
    first, second = select_stack(offsets, 0), select_stack(offsets, 1)
    keys, values = k[...], v[...]

    def back(keys, values, queries, grads):
        total_k = total_v = None
        for qq, gg in zip(queries, grads):
            qq = with_helpers(qq, gg)
            weight = jnp.exp2(nt(keys, qq) * EXP2)
            score = (weight * nt(values, gg)).astype(BF)
            part_k = nn(score, qq)
            part_v = nn(weight.astype(BF), gg)
            total_k = part_k if total_k is None else total_k + part_k
            total_v = part_v if total_v is None else total_v + part_v
        return total_k, total_v

    total_k = jnp.zeros((TOKENS, LANES), F32)
    total_v = jnp.zeros((TOKENS, LANES), F32)
    for h in range(HEADS):
        mask = head_mask(h, (1, LANES)).astype(BF)
        part_k, part_v = back(keys * mask, values * mask, (q[...], qp[...]), (gt[...], gp[...]))
        features = feature_mask(h, (TOKENS, LANES))
        total_k = jnp.where(features, part_k, total_k)
        total_v = jnp.where(features, part_v, total_v)
    k1 = masked_stack(nn(first, keys), ROWS1).astype(BF)
    v1 = masked_stack(nn(first, values), ROWS1).astype(BF)
    k2 = masked_stack(nn(second, keys), ROWS2).astype(BF)
    v2 = masked_stack(nn(second, values), ROWS2).astype(BF)
    k1_part, v1_part = back(k1, v1, (q1[...],), (g1[...],))
    k2_part, v2_part = back(k2, v2, (q2[...],), (g2[...],))
    total_k = (total_k + scatter_rows(offsets, k1_part, k2_part)) * SCALE
    total_v = total_v + scatter_rows(offsets, v1_part, v2_part)
    matrix = unpair_matrix()
    dk[...] = to_paired(total_k.astype(BF), matrix)
    dv[...] = to_paired(total_v.astype(BF), matrix)


def call(kernel, outs, n_smem, *args):
    return pl.pallas_call(
        kernel,
        out_shape=[jax.ShapeDtypeStruct(s, BF) for s in outs],
        in_specs=[SMEM] * n_smem + [VMEM] * (len(args) - n_smem),
        out_specs=[VMEM] * len(outs),
        compiler_params=pltpu.CompilerParams(vmem_limit_bytes=48 * 1024 * 1024),
    )(*args)


def per_device(queries, keys, values, grad_y, out_weight, counts, offsets):
    seq = lax.axis_index("seq")
    head = lax.axis_index("head")
    my_offsets = lax.dynamic_slice(offsets, (0, head * HEADS), (2, HEADS))
    my_count = lax.dynamic_slice(counts, (seq,), (1,))
    n_seq = lax.axis_size("seq")
    swap = [(i, i ^ 1) for i in range(n_seq)]
    rings = [[GROUP * b + i for i in range(GROUP)] for b in range(n_seq // GROUP)]
    planes = [[GROUP * b + i for b in range(n_seq // GROUP)] for i in range(GROUP)]

    def pair(x):
        return lax.ppermute(x, "seq", swap)

    def ring(x):
        copies = jnp.broadcast_to(x[None], (GROUP,) + x.shape)
        return lax.all_to_all(copies, "seq", 0, 0, axis_index_groups=rings).reshape((-1,) + x.shape[1:])

    def across(x):
        copies = jnp.broadcast_to(x[None], (GROUP,) + x.shape)
        return lax.all_to_all(copies, "seq", 0, 0, axis_index_groups=planes).reshape((-1,) + x.shape[1:])

    def gather_levels(rows1, rows2):
        both = ring(jnp.concatenate([rows1, rows2], axis=0)).reshape(GROUP, ROWS1 + ROWS2, -1)
        level1 = both[:, :ROWS1].reshape(GROUP * ROWS1, -1)
        level2 = across(both[:, ROWS1:].reshape(GROUP * ROWS2, -1))
        return level1, level2

    gy = lax.all_gather(grad_y, "head", axis=0)
    flat = (TOKENS, LANES)
    q, k, v, s1, s2 = call(
        prep_kernel, [flat, flat, flat, (ROWS1, 3 * LANES), (ROWS2, 3 * LANES)], 2, my_offsets, my_count, queries, keys, values
    )
    kvq1, kvq2 = gather_levels(s1, s2)
    q1, kv1 = kvq1[:, :LANES], kvq1[:, LANES:]
    q2, kv2 = kvq2[:, :LANES], kvq2[:, LANES:]
    kp, vp, qp = pair(k), pair(v), pair(q)
    (g,) = call(proj_kernel, [flat], 1, my_count, gy, out_weight)
    gt, g1, g2 = call(
        forward_kernel, [flat, (ROWS1, LANES), (ROWS2, LANES)], 1, my_offsets, q, g, k, v, kp, vp, kv1, kv2
    )
    gp = pair(gt)
    g1, g2 = gather_levels(g1, g2)
    paired = (HALF, 2 * FEAT)
    (dq,) = call(grad_query_kernel, [paired], 1, my_offsets, q, gt, k, v, kp, vp, kv1, kv2)
    dk, dv = call(grad_key_kernel, [paired, paired], 1, my_offsets, k, v, q, gt, qp, gp, q1, g1, q2, g2)
    return dq, dk, dv


def solution(mesh):
    split = P("seq", "head")
    return jax.shard_map(
        per_device,
        mesh=mesh,
        in_specs=(split, split, split, split, P("head", None), P(), P()),
        out_specs=(split, split, split),
        check_vma=False,
    )
```

```python
import math

import jax
import jax.numpy as jnp
from jax import lax
from jax.experimental import pallas as pl
from jax.experimental.pallas import tpu as pltpu
from jax.sharding import PartitionSpec as P

HEAD = 48
HEADS = 4
TOKENS = 256
HALF = TOKENS // 2
FEAT = HEADS * HEAD
PAIR = 2 * FEAT
LANES = 256
SIDE = 128
MID = 4
TOP = 16
GROUP = 8
ROWS1 = TOKENS // MID
ROWS2 = TOKENS // TOP
ROWS = ROWS1 + ROWS2
OWN = GROUP * ROWS1
TAIL = 2 * ROWS2 + 48
SCALE = HEAD**-0.5
ROOT = math.sqrt(HEAD)
EXP2 = SCALE * math.log2(math.e)
BIG = 1e30
VMEM_BYTES = 20 * 1024 * 1024
BF = jnp.bfloat16
F32 = jnp.float32

VMEM = pl.BlockSpec(memory_space=pltpu.VMEM)
SMEM = pl.BlockSpec(memory_space=pltpu.SMEM)


def iota(shape, dim):
    return lax.broadcasted_iota(jnp.int32, shape, dim)


def nt(a, b):
    return lax.dot_general(a, b, (((1,), (1,)), ((), ())), preferred_element_type=F32)


def nn(a, b):
    return jnp.dot(a, b, preferred_element_type=F32)


def first_mask(h, shape):
    lane = iota(shape, 1)
    return ((lane >= HEAD * h) & (lane < HEAD * (h + 1))) | ((lane >= FEAT + 8 * h) & (lane < FEAT + 8 * h + 8))


def second_mask(h, shape):
    lane = iota(shape, 1)
    at = lane - (LANES - FEAT)
    return ((at >= HEAD * h) & (at < HEAD * (h + 1))) | ((lane >= 8 * h) & (lane < 8 * h + 8))


def helper_mask(h, shape):
    lane = iota(shape, 1) & 63
    return (lane >= 8 * h) & (lane < 8 * h + 8)


def first_view(pair, helpers):
    left, right = pair[:, :SIDE], pair[:, SIDE:LANES]
    return jnp.concatenate([left, jnp.where(iota(right.shape, 1) < 64, right, helpers)], axis=1)


def second_view(pair, helpers):
    left, right = pair[:, SIDE:LANES], pair[:, LANES:]
    return jnp.concatenate([jnp.where(iota(left.shape, 1) < 64, helpers, left), right], axis=1)


def query_helpers(rows):
    lane = iota((rows, SIDE), 1)
    return jnp.where((lane >= 64) & (lane < 96) & ((lane & 7) == 3), 1.0, 0.0).astype(BF)


def key_helpers(mask):
    lane = iota(mask.shape, 1)
    slot = lane & 7
    used = (lane & 63) < 32
    value = jnp.where(slot < 3, -1.0, jnp.where(slot == 3, mask, jnp.where(slot < 7, -1.0, 0.0)))
    value = jnp.where((lane < 64) & (slot < 4), 0.0, value)
    value = jnp.where((lane >= 64) & (slot >= 4), 0.0, value)
    return jnp.where(used, value, 0.0).astype(BF)


def lane_offsets(offsets, level, shape):
    h = (iota(shape, 1) >> 3) & 3
    base = lax.axis_index("head") * HEADS
    at = [offsets[level, base + i] for i in range(HEADS)]
    return jnp.where(h == 0, at[0], jnp.where(h == 1, at[1], jnp.where(h == 2, at[2], at[3])))


def dilated_mask(offsets, level, count):
    rows, rate = (ROWS1, MID) if level == 0 else (ROWS2, TOP)
    shape = (rows, SIDE)
    return jnp.where(rate * iota(shape, 0) + lane_offsets(offsets, level, shape) < count, 0.0, -BIG)


def positions(shape):
    row = iota(shape, 0)
    return jnp.where(row < HALF, 2 * row, 2 * (row - HALF) + 1)


def full_mask(count):
    return jnp.where(positions((TOKENS, SIDE)) < count, 0.0, -BIG)


def by_parity(paired):
    halves = [
        jnp.concatenate([paired[:, (2 * h + t) * HEAD : (2 * h + t + 1) * HEAD] for h in range(HEADS)], axis=1)
        for t in range(2)
    ]
    return jnp.concatenate(halves, axis=0)


def to_paired(flat):
    pieces = []
    for h in range(HEADS):
        for t in range(2):
            pieces.append(flat[t * HALF : (t + 1) * HALF, h * HEAD : (h + 1) * HEAD])
    return jnp.concatenate(pieces, axis=1).astype(BF)


def place_of(offsets, level, h, shape, dim):
    rate = MID if level == 0 else TOP
    return rate * iota(shape, dim) + offsets[level, lax.axis_index("head") * HEADS + h]


def chosen(offsets, level, h, shape, dim):
    place = place_of(offsets, level, h, shape, dim)
    return ((place >> 1) + (place & 1) * HALF) == iota(shape, 1 - dim)


def select_stack(offsets, level):
    rows = ROWS1 if level == 0 else ROWS2
    return jnp.concatenate(
        [jnp.where(chosen(offsets, level, h, (rows, TOKENS), 0), 1.0, 0.0) for h in range(HEADS)], axis=0
    ).astype(BF)


def folded(stack, rows, mask):
    total = None
    for h in range(HEADS):
        part = jnp.where(mask(h, (rows, stack.shape[1])), stack[h * rows : (h + 1) * rows], 0.0)
        total = part if total is None else total + part
    return total


def head_stack(rows, mask):
    return jnp.concatenate([rows * mask(h, (1, rows.shape[1])).astype(BF) for h in range(HEADS)], axis=0)


def feature_mask(h, shape):
    lane = iota(shape, 1)
    return (lane >= HEAD * h) & (lane < HEAD * (h + 1))


def split3(x):
    high = x.astype(BF)
    rest = x - high.astype(F32)
    mid = rest.astype(BF)
    low = (rest - mid.astype(F32)).astype(BF)
    return high, mid, low


def paired_rows(offsets, source):
    parts = []
    for level, rows in ((0, ROWS1), (1, ROWS2)):
        total = None
        for h in range(HEADS):
            row = place_of(offsets, level, h, (rows, HALF), 0) >> 1
            pick = jnp.where(row == iota((rows, HALF), 1), 1.0, 0.0).astype(BF)
            both = nn(pick, source[:, 2 * HEAD * h : 2 * HEAD * (h + 1)])
            odd = (place_of(offsets, level, h, (rows, HEAD), 0) & 1) == 1
            part = jnp.where(odd, both[:, HEAD:], both[:, :HEAD])
            total = [part] if total is None else total + [part]
        parts.append(jnp.concatenate(total, axis=1))
    return jnp.concatenate(parts, axis=0)


def rows_kernel(offsets, k, v, copies):
    both = jnp.concatenate([paired_rows(offsets, k), paired_rows(offsets, v)], axis=1).astype(BF)
    for i in range(GROUP):
        copies[i] = both


def pairs_kernel(k, v, k_next, v_next, kv, kv_next):
    for a, b, out in ((k, v, kv), (k_next, v_next, kv_next)):
        out[...] = jnp.concatenate([by_parity(a[...].astype(F32)), by_parity(b[...].astype(F32))], axis=1).astype(BF)


def repeat_kernel(rows, out):
    block = rows[:, ROWS1:].reshape(GROUP * ROWS2, PAIR)
    for i in range(GROUP):
        out[i] = block


def proj_kernel(offsets, counts, gy, w, q, qg, qg_top):
    total = jnp.zeros((TOKENS, FEAT), F32)
    for i in range(4):
        flat = by_parity(gy[i].astype(F32)).astype(BF)
        total = total + nt(flat, w[:, i * FEAT : (i + 1) * FEAT])
    total = jnp.where(positions((TOKENS, FEAT)) < counts[lax.axis_index("seq")], total, 0.0)
    flat = jnp.concatenate([by_parity(q[...].astype(F32)), total], axis=1).astype(BF)
    qg[:TOKENS] = flat

    def mask(h, shape):
        return feature_mask(h, shape) | feature_mask(h + HEADS, shape)

    qg[TOKENS : TOKENS + ROWS1] = folded(nn(select_stack(offsets, 0), flat), ROWS1, mask).astype(BF)
    qg_top[...] = folded(nn(select_stack(offsets, 1), flat), ROWS2, mask).astype(BF)


def level_stats(keys, values, queries, grads):
    scores = [nt(k, queries) for k in keys]
    top = scores[0].max(axis=0, keepdims=True)
    for s in scores[1:]:
        top = jnp.maximum(top, s.max(axis=0, keepdims=True))
    mass = dot = None
    for s, v in zip(scores, values):
        e = jnp.exp2((s - top) * EXP2)
        part = e.sum(axis=0, keepdims=True)
        part_dot = (e * nt(v, grads)).sum(axis=0, keepdims=True)
        mass = part if mass is None else mass + part
        dot = part_dot if dot is None else dot + part_dot
    return top, mass, dot


def spread(stats, stack, rows):
    top, mass, dot = stats
    width = top.shape[1]
    lane = iota((HEADS, width), 1)
    row = iota((HEADS, width), 0)
    own = (lane >= rows * row) & (lane < rows * (row + 1))
    placed = [jnp.where(own, x, 0.0) for x in (top, mass, dot, jnp.ones_like(top))]
    placed = jnp.concatenate(placed, axis=0)
    out = sum(nn(term, stack) for term in split3(placed))
    there = out[12:16] > 0.5
    return jnp.where(there, out[0:4], -BIG), out[4:8], out[8:12]


def merged(parts):
    top = parts[0][0]
    for p in parts[1:]:
        top = jnp.maximum(top, p[0])
    mass = dot = 0.0
    for p in parts:
        f = jnp.exp2((p[0] - top) * EXP2)
        mass = mass + p[1] * f
        dot = dot + p[2] * f
    return top, mass, dot


def fill_level1(offsets, counts, rows, kv1):
    seq = lax.axis_index("seq")
    base = seq - (seq & (GROUP - 1))
    for s in range(GROUP):
        helpers = key_helpers(dilated_mask(offsets, 0, counts[base + s]))
        block = rows[s, :ROWS1]
        kv1[0, s * ROWS1 : (s + 1) * ROWS1] = first_view(block, helpers)
        kv1[1, s * ROWS1 : (s + 1) * ROWS1] = second_view(block, helpers)


def forward_kernel(offsets, counts, qg, qg_top, kv, kvp, rows, tail, kv1):
    seq = lax.axis_index("seq")
    fill_level1(offsets, counts, rows, kv1)
    flat = qg[:TOKENS]
    queries = first_view(flat, query_helpers(TOKENS))
    grads = second_view(flat, jnp.zeros((TOKENS, SIDE), BF))
    own = key_helpers(full_mask(counts[seq]))
    other = key_helpers(full_mask(counts[seq ^ 1]))
    keys = (first_view(kv[...], own), first_view(kvp[...], other))
    values = (second_view(kv[...], own), second_view(kvp[...], other))
    parts = []
    for h in range(HEADS):
        q_mask = first_mask(h, (1, LANES)).astype(BF)
        g_mask = second_mask(h, (1, LANES)).astype(BF)
        parts.append(level_stats(keys, values, queries * q_mask, grads * g_mask))
    level0 = [jnp.concatenate([p[i] for p in parts], axis=0) for i in range(3)]
    block = qg[TOKENS : TOKENS + ROWS1]
    q1 = head_stack(first_view(block, query_helpers(ROWS1)), first_mask)
    g1 = head_stack(second_view(block, jnp.zeros((ROWS1, SIDE), BF)), second_mask)
    select1, select2 = select_stack(offsets, 0), select_stack(offsets, 1)
    level1 = spread(level_stats((kv1[0],), (kv1[1],), q1, g1), select1, ROWS1)
    terms = split3(jnp.concatenate(merged((level0, level1)), axis=0))
    own_head = [(iota((3 * HEADS, 1), 0) & 3) == h for h in range(HEADS)]
    empty = jnp.zeros((3 * HEADS, SIDE - ROWS), F32)
    chosen_terms = []
    for term in terms:
        one, two = nt(term, select1), nt(term, select2)
        row1 = row2 = 0.0
        for h in range(HEADS):
            row1 = row1 + jnp.where(own_head[h], one[:, h * ROWS1 : (h + 1) * ROWS1], 0.0)
            row2 = row2 + jnp.where(own_head[h], two[:, h * ROWS2 : (h + 1) * ROWS2], 0.0)
        chosen_terms.append(jnp.concatenate([row1, row2, empty], axis=1))
    pad = jnp.zeros((16 - 3 * HEADS, PAIR), F32)
    tail[:ROWS2] = qg_top[...]
    tail[ROWS2 : 2 * ROWS2] = jnp.concatenate([jnp.concatenate(chosen_terms, axis=1), pad], axis=0).astype(BF)
    for i, term in enumerate(terms):
        wide = jnp.concatenate([term.astype(F32), jnp.zeros((3 * HEADS, PAIR - LANES), F32)], axis=1)
        tail[16 * (i + 2) : 16 * (i + 3)] = jnp.concatenate([wide, pad], axis=0).astype(BF)


def fill_level2(offsets, counts, rows, keys, values):
    for a in range(GROUP):
        for s in range(GROUP):
            helpers = key_helpers(dilated_mask(offsets, 1, counts[a * GROUP + s]))
            block = rows[a, s * ROWS2 : (s + 1) * ROWS2]
            at = (a * GROUP + s) * ROWS2
            keys[at : at + ROWS2] = first_view(block, helpers)
            values[at : at + ROWS2] = second_view(block, helpers)


def summed_terms(ref, at):
    wide = ref[at : at + 16].astype(F32)
    return wide[:, :SIDE] + wide[:, SIDE : 2 * SIDE] + wide[:, 2 * SIDE :]


def finish_kernel(offsets, counts, tails, rows, st, packed, keys, values):
    fill_level2(offsets, counts, rows, keys, values)
    starts = [0, TAIL] + [2 * TAIL + 2 * ROWS2 * i for i in range(GROUP - 2)]
    block = jnp.concatenate([tails[at : at + ROWS2] for at in starts], axis=0)
    width = GROUP * ROWS2
    q2 = head_stack(first_view(block, query_helpers(width)), first_mask)
    g2 = head_stack(second_view(block, jnp.zeros((width, SIDE), BF)), second_mask)
    flat = level_stats((keys[...],), (values[...],), q2, g2)
    level2 = [jnp.concatenate([x[:, h * width : (h + 1) * width] for h in range(HEADS)], axis=0) for x in flat]
    small = [summed_terms(tails, at + ROWS2) for at in starts]
    early1 = jnp.concatenate([x[:, :ROWS1] for x in small], axis=1)
    early2 = jnp.concatenate([x[:, ROWS1:ROWS] for x in small], axis=1)
    early0 = [
        sum(tails[at + 16 * i : at + 16 * (i + 1), :LANES].astype(F32) for i in range(2, 5)) for at in (0, TAIL)
    ]
    early = jnp.concatenate([early1, *early0], axis=1)
    total_rows = GROUP * ROWS1 + 2 * TOKENS
    shape = (width, total_rows)
    lane = iota(shape, 1)
    row = iota(shape, 0)
    ring = lane < GROUP * ROWS1
    inside = (lane - GROUP * ROWS1) & (TOKENS - 1)
    where0 = jnp.where(inside < HALF, 2 * inside, 2 * (inside - HALF) + 1)
    shard = jnp.where(ring, lane >> 6, (lane - GROUP * ROWS1) >> 8)
    same = shard == (row >> 4)
    head = lax.axis_index("head") * HEADS
    spread2 = []
    for h in range(HEADS):
        place = jnp.where(ring, MID * (lane & (ROWS1 - 1)) + offsets[0, head + h], where0)
        hit = same & (place == TOP * (row & (ROWS2 - 1)) + offsets[1, head + h])
        one_hot = jnp.where(hit, 1.0, 0.0).astype(BF)
        values_h = jnp.concatenate([x[h : h + 1] for x in level2] + [jnp.ones((1, width), F32)], axis=0)
        spread2.append(sum(nn(term, one_hot) for term in split3(values_h)))
    late = [jnp.concatenate([x[i : i + 1] for x in spread2], axis=0) for i in range(4)]
    late[0] = jnp.where(late[3] > 0.5, late[0], -BIG)
    first = merged(((early[0:4], early[4:8], early[8:12]), late[:3]))
    second = merged(((early2[0:4], early2[4:8], early2[8:12]), level2))
    top, total, dot = (jnp.concatenate([x, y], axis=1) for x, y in zip(first, second))
    grad_dot = dot / total
    log_total = top + jnp.log(total) * ROOT
    count = total_rows + width
    columns = jnp.concatenate(
        [x.astype(F32) for x in (*split3(log_total), *split3(grad_dot))]
        + [jnp.ones((HEADS, count), F32), jnp.zeros((HEADS, count), F32)],
        axis=0,
    )
    at = iota((8 * HEADS, SIDE), 0)
    s, h = at >> 2, at & 3
    slot = jnp.where(s < 3, s, jnp.where(s < 6, s + 1, jnp.where(s == 6, 3, 7)))
    place = jnp.where((iota((8 * HEADS, SIDE), 1) & 63) == 8 * h + slot, 1.0, 0.0).astype(BF)
    full = nn(columns.T.astype(BF), place).astype(BF)
    st[...] = full
    wide = jnp.concatenate([block, full[total_rows:]], axis=1)
    for n in range(GROUP):
        packed[n] = wide


def scatter_rows(offsets, parts1, parts2, shift):
    def mask(h, shape):
        lane = iota(shape, 1) - shift
        return (lane >= HEAD * h) & (lane < HEAD * (h + 1))

    total = None
    for level, part, rows in ((0, parts1, ROWS1), (1, parts2, ROWS2)):
        if part is None:
            continue
        place = jnp.concatenate(
            [jnp.where(chosen(offsets, level, h, (TOKENS, rows), 1), 1.0, 0.0) for h in range(HEADS)], axis=1
        ).astype(BF)
        part = jnp.concatenate(
            [jnp.where(mask(h, (rows, LANES)), part[h * rows : (h + 1) * rows], 0.0) for h in range(HEADS)], axis=0
        )
        high = part.astype(BF)
        low = (part - high.astype(F32)).astype(BF)
        got = nn(place, high) + nn(place, low)
        total = got if total is None else total + got
    return total


def grad_query_kernel(offsets, counts, qg, qg_top, st, kv, kvp, rows1, rows2, dq, kv1, keys2, values2):
    seq = lax.axis_index("seq")
    fill_level1(offsets, counts, rows1, kv1)
    fill_level2(offsets, counts, rows2, keys2, values2)
    own = key_helpers(full_mask(counts[seq]))
    other = key_helpers(full_mask(counts[seq ^ 1]))
    keys = (first_view(kv[...], own), first_view(kvp[...], other))
    values = (second_view(kv[...], own), second_view(kvp[...], other))

    def back(queries, grads, keys, values):
        total = None
        for kk, vv in zip(keys, values):
            weight = jnp.exp2(nt(queries, kk) * EXP2)
            score = (weight * nt(grads, vv)).astype(BF)
            part = nn(score, kk)
            total = part if total is None else total + part
        return total

    flat = qg[:TOKENS]
    mine = st[OWN : OWN + TOKENS]
    queries, grads = first_view(flat, mine), second_view(flat, mine)
    total = jnp.zeros((TOKENS, LANES), F32)
    for h in range(HEADS):
        q_mask = first_mask(h, (1, LANES)).astype(BF)
        g_mask = second_mask(h, (1, LANES)).astype(BF)
        part = back(queries * q_mask, grads * g_mask, keys, values)
        total = jnp.where(feature_mask(h, (TOKENS, LANES)), part, total)
    got = []
    for block, at, ks, vs in (
        (qg[TOKENS:], 0, kv1[0], kv1[1]),
        (qg_top[...], OWN + 2 * TOKENS, keys2[...], values2[...]),
    ):
        helpers = st[at : at + block.shape[0]]
        qs = head_stack(first_view(block, helpers), first_mask)
        gs = head_stack(second_view(block, helpers), second_mask)
        got.append(back(qs, gs, (ks,), (vs,)))
    total = (total + scatter_rows(offsets, got[0], got[1], 0)) * SCALE
    dq[...] = to_paired(total)


def key_back(keys, values, queries, grads):
    total_k = total_v = None
    for qq, gg in zip(queries, grads):
        weight = jnp.exp2(nt(keys, qq) * EXP2)
        score = (weight * nt(values, gg)).astype(BF)
        part_k = nn(score, qq)
        part_v = nn(weight.astype(BF), gg)
        total_k = part_k if total_k is None else total_k + part_k
        total_v = part_v if total_v is None else total_v + part_v
    return total_k, total_v


def grad_key_kernel(offsets, counts, kv, copies, qg, st, qgp, qg2, qg4, qg6, dk, dv, qs, gs):
    seq = lax.axis_index("seq")
    sources = ((qg, TOKENS), (qgp, TOKENS), *((ref, at) for ref in (qg2, qg4, qg6) for at in (0, ROWS1)))
    for i, (ref, at) in enumerate(sources):
        block = ref[at : at + ROWS1]
        helpers = st[i * ROWS1 : (i + 1) * ROWS1]
        qs[i * ROWS1 : (i + 1) * ROWS1] = first_view(block, helpers)
        gs[i * ROWS1 : (i + 1) * ROWS1] = second_view(block, helpers)
    own = key_helpers(full_mask(counts[seq]))
    keys, values = first_view(kv[...], own), second_view(kv[...], own)
    flat, other = qg[:TOKENS], qgp[:TOKENS]
    mine, next_st = st[OWN : OWN + TOKENS], st[OWN + TOKENS : OWN + 2 * TOKENS]
    queries = (first_view(flat, mine), first_view(other, next_st))
    grads = (second_view(flat, mine), second_view(other, next_st))
    total_k = jnp.zeros((TOKENS, LANES), F32)
    total_v = jnp.zeros((TOKENS, LANES), F32)
    for h in range(HEADS):
        k_mask = first_mask(h, (1, LANES)).astype(BF)
        v_mask = second_mask(h, (1, LANES)).astype(BF)
        part_k, part_v = key_back(keys * k_mask, values * v_mask, queries, grads)
        total_k = jnp.where(feature_mask(h, (TOKENS, LANES)), part_k, total_k)
        total_v = jnp.where(second_mask(h, (TOKENS, LANES)), part_v, total_v)
    helpers = key_helpers(dilated_mask(offsets, 0, counts[seq]))
    block = copies[0, :ROWS1]
    k1 = head_stack(first_view(block, helpers), first_mask)
    v1 = head_stack(second_view(block, helpers), second_mask)
    k1_part, v1_part = key_back(k1, v1, (qs[...],), (gs[...],))
    dk[...] = total_k + scatter_rows(offsets, k1_part, None, 0)
    dv[...] = total_v + scatter_rows(offsets, v1_part, None, LANES - FEAT)


def last_kernel(offsets, counts, rows, qg2, dk_in, dv_in, dk, dv):
    seq = lax.axis_index("seq")
    full = qg2[...].reshape(GROUP * GROUP * ROWS2, PAIR + SIDE)
    helpers = full[:, PAIR:]
    queries, grads = first_view(full[:, :PAIR], helpers), second_view(full[:, :PAIR], helpers)
    mine = key_helpers(dilated_mask(offsets, 1, counts[seq]))
    block = rows[0, ROWS1:]
    k2 = head_stack(first_view(block, mine), first_mask)
    v2 = head_stack(second_view(block, mine), second_mask)
    k2_part, v2_part = key_back(k2, v2, (queries,), (grads,))
    total_k = (dk_in[...] + scatter_rows(offsets, None, k2_part, 0)) * SCALE
    total_v = dv_in[...] + scatter_rows(offsets, None, v2_part, LANES - FEAT)
    dk[...] = to_paired(total_k)
    dv[...] = to_paired(total_v[:, LANES - FEAT :])


def call(kernel, outs, n_smem, *args, scratch=()):
    return pl.pallas_call(
        kernel,
        out_shape=[jax.ShapeDtypeStruct(s, d) for s, d in outs],
        in_specs=[SMEM] * n_smem + [VMEM] * (len(args) - n_smem),
        out_specs=[VMEM] * len(outs),
        scratch_shapes=[pltpu.VMEM(s, BF) for s in scratch],
        compiler_params=pltpu.CompilerParams(vmem_limit_bytes=VMEM_BYTES),
    )(*args)


def per_device(queries, keys, values, grad_y, out_weight, counts, offsets):
    n_seq = lax.axis_size("seq")
    rings = [[GROUP * b + i for i in range(GROUP)] for b in range(n_seq // GROUP)]
    planes = [[GROUP * b + i for b in range(n_seq // GROUP)] for i in range(GROUP)]

    def swap(x, bits):
        return lax.ppermute(x, "seq", [(i, i ^ bits) for i in range(n_seq)])

    def shift(x, step):
        return lax.ppermute(x, "seq", [(r[i], r[(i + step) % GROUP]) for r in rings for i in range(GROUP)])

    def exchange(copies, groups):
        return lax.all_to_all(copies, "seq", 0, 0, axis_index_groups=groups)

    def far(own, near):
        both = jnp.concatenate([own, near], axis=0)
        return tuple(shift(both, step) for step in (2, 4, 6))

    k_next, v_next = swap(keys, 1), swap(values, 1)
    (copies,) = call(rows_kernel, [((GROUP, ROWS, PAIR), BF)], 1, offsets, keys, values)
    copies, k_next, v_next = lax.optimization_barrier((copies, k_next, v_next))
    ring_kv = exchange(copies, rings)
    flat = (TOKENS, PAIR)
    kv, kvp = call(pairs_kernel, [(flat, BF)] * 2, 0, keys, values, k_next, v_next)
    gy = lax.all_gather(grad_y, "head", axis=0)
    qg, qg_top = call(
        proj_kernel, [((TOKENS + ROWS1, PAIR), BF), ((ROWS2, PAIR), BF)], 2, offsets, counts, gy, out_weight, queries
    )
    qgp = swap(qg, 1)
    (tail,) = call(
        forward_kernel, [((TAIL, PAIR), BF)], 2, offsets, counts, qg, qg_top, kv, kvp, ring_kv,
        scratch=[(2, GROUP * ROWS1, LANES)],
    )
    ring_kv, tail = lax.optimization_barrier((ring_kv, tail))
    tail_next = swap(tail, 1)
    (repeated,) = call(repeat_kernel, [((GROUP, GROUP * ROWS2, PAIR), BF)], 0, ring_kv)
    all_kv = exchange(repeated, planes)
    tails = far(tail[: 2 * ROWS2], tail_next[: 2 * ROWS2])
    tails, qgp = lax.optimization_barrier((jnp.concatenate([tail, tail_next, *tails], axis=0), qgp))
    big = (GROUP * GROUP * ROWS2, LANES)
    st_rows = OWN + 2 * TOKENS + GROUP * ROWS2
    st, packed = call(
        finish_kernel, [((st_rows, SIDE), BF), ((GROUP, GROUP * ROWS2, PAIR + SIDE), BF)], 2, offsets, counts,
        tails, all_kv, scratch=[big, big],
    )
    qgs = far(qg[TOKENS:], qgp[TOKENS:])
    all_qg = exchange(packed, planes)
    (dq,) = call(
        grad_query_kernel, [((HALF, PAIR), BF)], 2, offsets, counts, qg, qg_top, st, kv, kvp, ring_kv, all_kv,
        scratch=[(2, GROUP * ROWS1, LANES), big, big],
    )
    dk, dv = call(
        grad_key_kernel, [((TOKENS, LANES), F32)] * 2, 2, offsets, counts, kv, copies, qg, st, qgp, *qgs,
        scratch=[(GROUP * ROWS1, LANES)] * 2,
    )
    dk, dv = call(last_kernel, [((HALF, PAIR), BF)] * 2, 2, offsets, counts, copies, all_qg, dk, dv)
    return dq, dk, dv


def solution(mesh):
    split = P("seq", "head")
    return jax.shard_map(
        per_device,
        mesh=mesh,
        in_specs=(split, split, split, split, P("head", None), P(), P()),
        out_specs=(split, split, split),
        check_vma=False,
    )
```

```python
import math

import jax
import jax.numpy as jnp
from jax import lax
from jax.experimental import pallas as pl
from jax.experimental.pallas import tpu as pltpu
from jax.sharding import PartitionSpec as P

HEAD = 48
HEADS = 4
TOKENS = 256
HALF = TOKENS // 2
FEAT = HEADS * HEAD
PAIR = 2 * FEAT
LANES = 256
SIDE = 128
MID = 4
TOP = 16
GROUP = 8
ROWS1 = TOKENS // MID
ROWS2 = TOKENS // TOP
ROWS = ROWS1 + ROWS2
OWN = GROUP * ROWS1
TAIL = 2 * ROWS2 + 48
SCALE = HEAD**-0.5
ROOT = math.sqrt(HEAD)
EXP2 = SCALE * math.log2(math.e)
BIG = 1e30
VMEM_BYTES = 20 * 1024 * 1024
BF = jnp.bfloat16
F32 = jnp.float32

VMEM = pl.BlockSpec(memory_space=pltpu.VMEM)
SMEM = pl.BlockSpec(memory_space=pltpu.SMEM)


def iota(shape, dim):
    return lax.broadcasted_iota(jnp.int32, shape, dim)


def nt(a, b):
    return lax.dot_general(a, b, (((1,), (1,)), ((), ())), preferred_element_type=F32)


def nn(a, b):
    return jnp.dot(a, b, preferred_element_type=F32)


def first_mask(h, shape):
    lane = iota(shape, 1)
    return ((lane >= HEAD * h) & (lane < HEAD * (h + 1))) | ((lane >= FEAT + 8 * h) & (lane < FEAT + 8 * h + 8))


def second_mask(h, shape):
    lane = iota(shape, 1)
    at = lane - (LANES - FEAT)
    return ((at >= HEAD * h) & (at < HEAD * (h + 1))) | ((lane >= 8 * h) & (lane < 8 * h + 8))


def helper_mask(h, shape):
    lane = iota(shape, 1) & 63
    return (lane >= 8 * h) & (lane < 8 * h + 8)


def first_view(pair, helpers):
    left, right = pair[:, :SIDE], pair[:, SIDE:LANES]
    return jnp.concatenate([left, jnp.where(iota(right.shape, 1) < 64, right, helpers)], axis=1)


def second_view(pair, helpers):
    left, right = pair[:, SIDE:LANES], pair[:, LANES:]
    return jnp.concatenate([jnp.where(iota(left.shape, 1) < 64, helpers, left), right], axis=1)


def query_helpers(rows):
    lane = iota((rows, SIDE), 1)
    return jnp.where((lane >= 64) & (lane < 96) & ((lane & 7) == 3), 1.0, 0.0).astype(BF)


def key_helpers(mask):
    lane = iota(mask.shape, 1)
    slot = lane & 7
    used = (lane & 63) < 32
    value = jnp.where(slot < 3, -1.0, jnp.where(slot == 3, mask, jnp.where(slot < 7, -1.0, 0.0)))
    value = jnp.where((lane < 64) & (slot < 4), 0.0, value)
    value = jnp.where((lane >= 64) & (slot >= 4), 0.0, value)
    return jnp.where(used, value, 0.0).astype(BF)


def lane_offsets(offsets, level, shape):
    h = (iota(shape, 1) >> 3) & 3
    base = lax.axis_index("head") * HEADS
    at = [offsets[level, base + i] for i in range(HEADS)]
    return jnp.where(h == 0, at[0], jnp.where(h == 1, at[1], jnp.where(h == 2, at[2], at[3])))


def dilated_mask(offsets, level, count):
    rows, rate = (ROWS1, MID) if level == 0 else (ROWS2, TOP)
    shape = (rows, SIDE)
    return jnp.where(rate * iota(shape, 0) + lane_offsets(offsets, level, shape) < count, 0.0, -BIG)


def positions(shape):
    row = iota(shape, 0)
    return jnp.where(row < HALF, 2 * row, 2 * (row - HALF) + 1)


def full_mask(count):
    return jnp.where(positions((TOKENS, SIDE)) < count, 0.0, -BIG)


def by_parity(paired):
    halves = [
        jnp.concatenate([paired[:, (2 * h + t) * HEAD : (2 * h + t + 1) * HEAD] for h in range(HEADS)], axis=1)
        for t in range(2)
    ]
    return jnp.concatenate(halves, axis=0)


def to_paired(flat):
    flat = flat.astype(BF)
    pieces = []
    for h in range(HEADS):
        for t in range(2):
            pieces.append(flat[t * HALF : (t + 1) * HALF, h * HEAD : (h + 1) * HEAD])
    return jnp.concatenate(pieces, axis=1)


def place_of(offsets, level, h, shape, dim):
    rate = MID if level == 0 else TOP
    return rate * iota(shape, dim) + offsets[level, lax.axis_index("head") * HEADS + h]


def chosen(offsets, level, h, shape, dim):
    place = place_of(offsets, level, h, shape, dim)
    return ((place >> 1) + (place & 1) * HALF) == iota(shape, 1 - dim)


def select_stack(offsets, level):
    rows = ROWS1 if level == 0 else ROWS2
    return jnp.concatenate(
        [jnp.where(chosen(offsets, level, h, (rows, TOKENS), 0), 1.0, 0.0) for h in range(HEADS)], axis=0
    ).astype(BF)


def folded(stack, rows, mask):
    total = None
    for h in range(HEADS):
        part = jnp.where(mask(h, (rows, stack.shape[1])), stack[h * rows : (h + 1) * rows], 0.0)
        total = part if total is None else total + part
    return total


def head_stack(rows, mask):
    return jnp.concatenate([rows * mask(h, (1, rows.shape[1])).astype(BF) for h in range(HEADS)], axis=0)


def feature_mask(h, shape):
    lane = iota(shape, 1)
    return (lane >= HEAD * h) & (lane < HEAD * (h + 1))


def split3(x):
    high = x.astype(BF)
    rest = x - high.astype(F32)
    mid = rest.astype(BF)
    low = (rest - mid.astype(F32)).astype(BF)
    return high, mid, low


def paired_rows(offsets, source):
    parts = []
    for level, rows in ((0, ROWS1), (1, ROWS2)):
        total = None
        for h in range(HEADS):
            row = place_of(offsets, level, h, (rows, HALF), 0) >> 1
            pick = jnp.where(row == iota((rows, HALF), 1), 1.0, 0.0).astype(BF)
            both = nn(pick, source[:, 2 * HEAD * h : 2 * HEAD * (h + 1)])
            odd = (place_of(offsets, level, h, (rows, HEAD), 0) & 1) == 1
            part = jnp.where(odd, both[:, HEAD:], both[:, :HEAD])
            total = [part] if total is None else total + [part]
        parts.append(jnp.concatenate(total, axis=1))
    return jnp.concatenate(parts, axis=0)


def rows_kernel(offsets, k, v, copies):
    both = jnp.concatenate([paired_rows(offsets, k), paired_rows(offsets, v)], axis=1).astype(BF)
    for i in range(GROUP):
        copies[i] = both


def pairs_kernel(k, v, k_next, v_next, kv, kv_next):
    for a, b, out in ((k, v, kv), (k_next, v_next, kv_next)):
        out[...] = jnp.concatenate([by_parity(a[...]), by_parity(b[...])], axis=1)


def repeat_kernel(rows, out):
    block = rows[:, ROWS1:].reshape(GROUP * ROWS2, PAIR)
    for i in range(GROUP):
        out[i] = block


def proj_kernel(offsets, counts, gy, w, q, qg, qg_top):
    total = jnp.zeros((TOKENS, FEAT), F32)
    for i in range(4):
        flat = by_parity(gy[i])
        total = total + nt(flat, w[:, i * FEAT : (i + 1) * FEAT])
    total = jnp.where(positions((TOKENS, FEAT)) < counts[lax.axis_index("seq")], total, 0.0)
    flat = jnp.concatenate([by_parity(q[...]), total.astype(BF)], axis=1)
    qg[:TOKENS] = flat

    def mask(h, shape):
        return feature_mask(h, shape) | feature_mask(h + HEADS, shape)

    qg[TOKENS : TOKENS + ROWS1] = folded(nn(select_stack(offsets, 0), flat), ROWS1, mask).astype(BF)
    qg_top[...] = folded(nn(select_stack(offsets, 1), flat), ROWS2, mask).astype(BF)


def level_stats(keys, values, queries, grads):
    scores = [nt(k, queries) for k in keys]
    top = scores[0].max(axis=0, keepdims=True)
    for s in scores[1:]:
        top = jnp.maximum(top, s.max(axis=0, keepdims=True))
    mass = dot = None
    for s, v in zip(scores, values):
        e = jnp.exp2((s - top) * EXP2)
        part = e.sum(axis=0, keepdims=True)
        part_dot = (e * nt(v, grads)).sum(axis=0, keepdims=True)
        mass = part if mass is None else mass + part
        dot = part_dot if dot is None else dot + part_dot
    return top, mass, dot


def spread(stats, stack, rows):
    top, mass, dot = stats
    width = top.shape[1]
    lane = iota((HEADS, width), 1)
    row = iota((HEADS, width), 0)
    own = (lane >= rows * row) & (lane < rows * (row + 1))
    placed = [jnp.where(own, x, 0.0) for x in (top, mass, dot, jnp.ones_like(top))]
    placed = jnp.concatenate(placed, axis=0)
    out = sum(nn(term, stack) for term in split3(placed))
    there = out[12:16] > 0.5
    return jnp.where(there, out[0:4], -BIG), out[4:8], out[8:12]


def merged(parts):
    top = parts[0][0]
    for p in parts[1:]:
        top = jnp.maximum(top, p[0])
    mass = dot = 0.0
    for p in parts:
        f = jnp.exp2((p[0] - top) * EXP2)
        mass = mass + p[1] * f
        dot = dot + p[2] * f
    return top, mass, dot


def fill_level1(offsets, counts, rows, kv1):
    seq = lax.axis_index("seq")
    base = seq - (seq & (GROUP - 1))
    for s in range(GROUP):
        helpers = key_helpers(dilated_mask(offsets, 0, counts[base + s]))
        block = rows[s, :ROWS1]
        kv1[0, s * ROWS1 : (s + 1) * ROWS1] = first_view(block, helpers)
        kv1[1, s * ROWS1 : (s + 1) * ROWS1] = second_view(block, helpers)


def by_head(x, width):
    return jnp.concatenate([x[:, h * width : (h + 1) * width] for h in range(HEADS)], axis=0)


def level0_kernel(counts, qg, kv, kvp, stats):
    seq = lax.axis_index("seq")
    flat = qg[:TOKENS]
    queries = head_stack(first_view(flat, query_helpers(TOKENS)), first_mask)
    grads = head_stack(second_view(flat, jnp.zeros((TOKENS, SIDE), BF)), second_mask)
    own = key_helpers(full_mask(counts[seq]))
    other = key_helpers(full_mask(counts[seq ^ 1]))
    keys = (first_view(kv[...], own), first_view(kvp[...], other))
    values = (second_view(kv[...], own), second_view(kvp[...], other))
    for i, x in enumerate(level_stats(keys, values, queries, grads)):
        stats[4 * i : 4 * i + 4] = by_head(x, TOKENS)
    stats[12:16] = jnp.zeros((4, TOKENS), F32)


def level1_kernel(offsets, counts, qg, qg_top, rows, stats, tail, kv1):
    fill_level1(offsets, counts, rows, kv1)
    level0 = (stats[0:4], stats[4:8], stats[8:12])
    block = qg[TOKENS : TOKENS + ROWS1]
    q1 = head_stack(first_view(block, query_helpers(ROWS1)), first_mask)
    g1 = head_stack(second_view(block, jnp.zeros((ROWS1, SIDE), BF)), second_mask)
    select1, select2 = select_stack(offsets, 0), select_stack(offsets, 1)
    level1 = spread(level_stats((kv1[0],), (kv1[1],), q1, g1), select1, ROWS1)
    terms = split3(jnp.concatenate(merged((level0, level1)), axis=0))
    own_head = [(iota((3 * HEADS, 1), 0) & 3) == h for h in range(HEADS)]
    empty = jnp.zeros((3 * HEADS, SIDE - ROWS), F32)
    chosen_terms = []
    for term in terms:
        one, two = nt(term, select1), nt(term, select2)
        row1 = row2 = 0.0
        for h in range(HEADS):
            row1 = row1 + jnp.where(own_head[h], one[:, h * ROWS1 : (h + 1) * ROWS1], 0.0)
            row2 = row2 + jnp.where(own_head[h], two[:, h * ROWS2 : (h + 1) * ROWS2], 0.0)
        chosen_terms.append(jnp.concatenate([row1, row2, empty], axis=1))
    pad = jnp.zeros((16 - 3 * HEADS, PAIR), F32)
    tail[:ROWS2] = qg_top[...]
    tail[ROWS2 : 2 * ROWS2] = jnp.concatenate([jnp.concatenate(chosen_terms, axis=1), pad], axis=0).astype(BF)
    for i, term in enumerate(terms):
        wide = jnp.concatenate([term.astype(F32), jnp.zeros((3 * HEADS, PAIR - LANES), F32)], axis=1)
        tail[16 * (i + 2) : 16 * (i + 3)] = jnp.concatenate([wide, pad], axis=0).astype(BF)


def fill_level2(offsets, counts, rows, keys, values):
    for a in range(GROUP):
        for s in range(GROUP):
            helpers = key_helpers(dilated_mask(offsets, 1, counts[a * GROUP + s]))
            block = rows[a, s * ROWS2 : (s + 1) * ROWS2]
            at = (a * GROUP + s) * ROWS2
            keys[at : at + ROWS2] = first_view(block, helpers)
            values[at : at + ROWS2] = second_view(block, helpers)


def summed_terms(ref, at):
    wide = ref[at : at + 16].astype(F32)
    return wide[:, :SIDE] + wide[:, SIDE : 2 * SIDE] + wide[:, 2 * SIDE :]


def finish_kernel(offsets, counts, tails, rows, st1, st, packed, keys, values):
    fill_level2(offsets, counts, rows, keys, values)
    starts = [0, TAIL] + [2 * TAIL + 2 * ROWS2 * i for i in range(GROUP - 2)]
    block = jnp.concatenate([tails[at : at + ROWS2] for at in starts], axis=0)
    width = GROUP * ROWS2
    q2 = head_stack(first_view(block, query_helpers(width)), first_mask)
    g2 = head_stack(second_view(block, jnp.zeros((width, SIDE), BF)), second_mask)
    flat = level_stats((keys[...],), (values[...],), q2, g2)
    level2 = [by_head(x, width) for x in flat]
    small = [summed_terms(tails, at + ROWS2) for at in starts]
    early1 = jnp.concatenate([x[:, :ROWS1] for x in small], axis=1)
    early2 = jnp.concatenate([x[:, ROWS1:ROWS] for x in small], axis=1)
    early0 = [
        sum(tails[at + 16 * i : at + 16 * (i + 1), :LANES].astype(F32) for i in range(2, 5)) for at in (0, TAIL)
    ]
    early = jnp.concatenate([early1, *early0], axis=1)
    total_rows = GROUP * ROWS1 + 2 * TOKENS
    shape = (width, total_rows)
    lane = iota(shape, 1)
    row = iota(shape, 0)
    ring = lane < GROUP * ROWS1
    inside = (lane - GROUP * ROWS1) & (TOKENS - 1)
    where0 = jnp.where(inside < HALF, 2 * inside, 2 * (inside - HALF) + 1)
    shard = jnp.where(ring, lane >> 6, (lane - GROUP * ROWS1) >> 8)
    same = shard == (row >> 4)
    head = lax.axis_index("head") * HEADS
    spread2 = []
    for h in range(HEADS):
        place = jnp.where(ring, MID * (lane & (ROWS1 - 1)) + offsets[0, head + h], where0)
        hit = same & (place == TOP * (row & (ROWS2 - 1)) + offsets[1, head + h])
        one_hot = jnp.where(hit, 1.0, 0.0).astype(BF)
        values_h = jnp.concatenate([x[h : h + 1] for x in level2] + [jnp.ones((1, width), F32)], axis=0)
        spread2.append(sum(nn(term, one_hot) for term in split3(values_h)))
    late = [jnp.concatenate([x[i : i + 1] for x in spread2], axis=0) for i in range(4)]
    late[0] = jnp.where(late[3] > 0.5, late[0], -BIG)
    first = merged(((early[0:4], early[4:8], early[8:12]), late[:3]))
    second = merged(((early2[0:4], early2[4:8], early2[8:12]), level2))
    top, total, dot = (jnp.concatenate([x, y], axis=1) for x, y in zip(first, second))
    grad_dot = dot / total
    log_total = top + jnp.log(total) * ROOT
    count = total_rows + width
    columns = jnp.concatenate(
        [x.astype(F32) for x in (*split3(log_total), *split3(grad_dot))]
        + [jnp.ones((HEADS, count), F32), jnp.zeros((HEADS, count), F32)],
        axis=0,
    )
    at = iota((8 * HEADS, SIDE), 0)
    s, h = at >> 2, at & 3
    slot = jnp.where(s < 3, s, jnp.where(s < 6, s + 1, jnp.where(s == 6, 3, 7)))
    place = jnp.where((iota((8 * HEADS, SIDE), 1) & 63) == 8 * h + slot, 1.0, 0.0).astype(BF)
    full = nn(columns.T.astype(BF), place).astype(BF)
    st1[...] = full[:OWN]
    st[...] = full[OWN:]
    wide = jnp.concatenate([block, full[total_rows:]], axis=1)
    for n in range(GROUP):
        packed[n] = wide


def scatter_rows(offsets, parts1, parts2, shift):
    def mask(h, shape):
        lane = iota(shape, 1) - shift
        return (lane >= HEAD * h) & (lane < HEAD * (h + 1))

    total = None
    for level, part, rows in ((0, parts1, ROWS1), (1, parts2, ROWS2)):
        if part is None:
            continue
        place = jnp.concatenate(
            [jnp.where(chosen(offsets, level, h, (TOKENS, rows), 1), 1.0, 0.0) for h in range(HEADS)], axis=1
        ).astype(BF)
        part = jnp.concatenate(
            [jnp.where(mask(h, (rows, LANES)), part[h * rows : (h + 1) * rows], 0.0) for h in range(HEADS)], axis=0
        )
        high = part.astype(BF)
        low = (part - high.astype(F32)).astype(BF)
        got = nn(place, high) + nn(place, low)
        total = got if total is None else total + got
    return total


def grad_query_kernel(offsets, counts, qg, qg_top, st1, st, kv, kvp, rows1, rows2, dq, kv1, keys2, values2):
    seq = lax.axis_index("seq")
    fill_level1(offsets, counts, rows1, kv1)
    fill_level2(offsets, counts, rows2, keys2, values2)
    own = key_helpers(full_mask(counts[seq]))
    other = key_helpers(full_mask(counts[seq ^ 1]))
    keys = (first_view(kv[...], own), first_view(kvp[...], other))
    values = (second_view(kv[...], own), second_view(kvp[...], other))

    def back(queries, grads, keys, values):
        total = None
        for kk, vv in zip(keys, values):
            weight = jnp.exp2(nt(queries, kk) * EXP2)
            score = (weight * nt(grads, vv)).astype(BF)
            part = nn(score, kk)
            total = part if total is None else total + part
        return total

    flat = qg[:TOKENS]
    mine = st[:TOKENS]
    queries, grads = first_view(flat, mine), second_view(flat, mine)
    part = back(head_stack(queries, first_mask), head_stack(grads, second_mask), keys, values)
    total = folded(part, TOKENS, feature_mask)
    got = []
    for block, helpers, ks, vs in (
        (qg[TOKENS:], st1[:ROWS1], kv1[0], kv1[1]),
        (qg_top[...], st[2 * TOKENS : 2 * TOKENS + ROWS2], keys2[...], values2[...]),
    ):
        qs = head_stack(first_view(block, helpers), first_mask)
        gs = head_stack(second_view(block, helpers), second_mask)
        got.append(back(qs, gs, (ks,), (vs,)))
    total = (total + scatter_rows(offsets, got[0], got[1], 0)) * SCALE
    dq[...] = to_paired(total)


def key_back(keys, values, queries, grads):
    total_k = total_v = None
    for qq, gg in zip(queries, grads):
        weight = jnp.exp2(nt(keys, qq) * EXP2)
        score = (weight * nt(values, gg)).astype(BF)
        part_k = nn(score, qq)
        part_v = nn(weight.astype(BF), gg)
        total_k = part_k if total_k is None else total_k + part_k
        total_v = part_v if total_v is None else total_v + part_v
    return total_k, total_v


def grad_key_kernel(counts, kv, qg, st, qgp, out):
    own = key_helpers(full_mask(counts[lax.axis_index("seq")]))
    keys, values = first_view(kv[...], own), second_view(kv[...], own)
    flat, other = qg[:TOKENS], qgp[:TOKENS]
    mine, next_st = st[:TOKENS], st[TOKENS : 2 * TOKENS]
    queries = (first_view(flat, mine), first_view(other, next_st))
    grads = (second_view(flat, mine), second_view(other, next_st))
    part_k, part_v = key_back(head_stack(keys, first_mask), head_stack(values, second_mask), queries, grads)
    out[:, :FEAT] = folded(part_k, TOKENS, feature_mask)[:, :FEAT]
    out[:, FEAT:] = folded(part_v, TOKENS, second_mask)[:, LANES - FEAT :]


def level1_keys_kernel(offsets, counts, copies, near, far2, far4, far6, st1, level0, out, qs, gs):
    for i in range(GROUP):
        block = (near, far2, far4, far6)[i // 2][(i & 1) * ROWS1 : (i & 1) * ROWS1 + ROWS1]
        helpers = st1[i * ROWS1 : (i + 1) * ROWS1]
        qs[i * ROWS1 : (i + 1) * ROWS1] = first_view(block, helpers)
        gs[i * ROWS1 : (i + 1) * ROWS1] = second_view(block, helpers)
    mine = key_helpers(dilated_mask(offsets, 0, counts[lax.axis_index("seq")]))
    block = copies[0, :ROWS1]
    k1 = head_stack(first_view(block, mine), first_mask)
    v1 = head_stack(second_view(block, mine), second_mask)
    k1_part, v1_part = key_back(k1, v1, (qs[...],), (gs[...],))
    out[:, :FEAT] = level0[:, :FEAT] + scatter_rows(offsets, k1_part, None, 0)[:, :FEAT]
    out[:, FEAT:] = level0[:, FEAT:] + scatter_rows(offsets, v1_part, None, LANES - FEAT)[:, LANES - FEAT :]


def last_kernel(offsets, counts, copies, all_qg, early, dk, dv):
    full = all_qg[...].reshape(GROUP * GROUP * ROWS2, PAIR + SIDE)
    helpers = full[:, PAIR:]
    queries, grads = first_view(full[:, :PAIR], helpers), second_view(full[:, :PAIR], helpers)
    mine = key_helpers(dilated_mask(offsets, 1, counts[lax.axis_index("seq")]))
    block = copies[0, ROWS1:]
    k2 = head_stack(first_view(block, mine), first_mask)
    v2 = head_stack(second_view(block, mine), second_mask)
    k2_part, v2_part = key_back(k2, v2, (queries,), (grads,))
    dk[...] = to_paired((early[:, :FEAT] + scatter_rows(offsets, None, k2_part, 0)[:, :FEAT]) * SCALE)
    dv[...] = to_paired(early[:, FEAT:] + scatter_rows(offsets, None, v2_part, LANES - FEAT)[:, LANES - FEAT :])


def call(kernel, outs, n_smem, *args, scratch=()):
    return pl.pallas_call(
        kernel,
        out_shape=[jax.ShapeDtypeStruct(s, d) for s, d in outs],
        in_specs=[SMEM] * n_smem + [VMEM] * (len(args) - n_smem),
        out_specs=[VMEM] * len(outs),
        scratch_shapes=[pltpu.VMEM(s, BF) for s in scratch],
        compiler_params=pltpu.CompilerParams(vmem_limit_bytes=VMEM_BYTES),
    )(*args)


def per_device(queries, keys, values, grad_y, out_weight, counts, offsets):
    n_seq = lax.axis_size("seq")
    rings = [[GROUP * b + i for i in range(GROUP)] for b in range(n_seq // GROUP)]
    planes = [[GROUP * b + i for b in range(n_seq // GROUP)] for i in range(GROUP)]

    def swap(x, bits):
        return lax.ppermute(x, "seq", [(i, i ^ bits) for i in range(n_seq)])

    def shift(x, step):
        return lax.ppermute(x, "seq", [(r[i], r[(i + step) % GROUP]) for r in rings for i in range(GROUP)])

    def exchange(copies, groups):
        return lax.all_to_all(copies, "seq", 0, 0, axis_index_groups=groups)

    def far(own, near):
        both = jnp.concatenate([own, near], axis=0)
        return tuple(shift(both, step) for step in (2, 4, 6))

    k_next, v_next = swap(keys, 1), swap(values, 1)
    (copies,) = call(rows_kernel, [((GROUP, ROWS, PAIR), BF)], 1, offsets, keys, values)
    copies, k_next, v_next = lax.optimization_barrier((copies, k_next, v_next))
    ring_kv = exchange(copies, rings)
    flat = (TOKENS, PAIR)
    kv, kvp = call(pairs_kernel, [(flat, BF)] * 2, 0, keys, values, k_next, v_next)
    gy = lax.all_gather(grad_y, "head", axis=0)
    qg, qg_top = call(
        proj_kernel, [((TOKENS + ROWS1, PAIR), BF), ((ROWS2, PAIR), BF)], 2, offsets, counts, gy, out_weight, queries
    )
    qgp = swap(qg, 1)
    (stats,) = call(level0_kernel, [((16, TOKENS), F32)], 1, counts, qg, kv, kvp)
    ring_kv, stats = lax.optimization_barrier((ring_kv, stats))
    (tail,) = call(
        level1_kernel, [((TAIL, PAIR), BF)], 2, offsets, counts, qg, qg_top, ring_kv, stats,
        scratch=[(2, GROUP * ROWS1, LANES)],
    )
    tail_next = swap(tail, 1)
    ring_kv, tail_next, qgp = lax.optimization_barrier((ring_kv, tail_next, qgp))
    (repeated,) = call(repeat_kernel, [((GROUP, GROUP * ROWS2, PAIR), BF)], 0, ring_kv)
    all_kv = exchange(repeated, planes)
    tails = far(tail[: 2 * ROWS2], tail_next[: 2 * ROWS2])
    tails, qgp = lax.optimization_barrier((jnp.concatenate([tail, tail_next, *tails], axis=0), qgp))
    big = (GROUP * GROUP * ROWS2, LANES)
    st_rows = 2 * TOKENS + GROUP * ROWS2
    st1, st, packed = call(
        finish_kernel, [((OWN, SIDE), BF), ((st_rows, SIDE), BF), ((GROUP, GROUP * ROWS2, PAIR + SIDE), BF)], 2, offsets, counts,
        tails, all_kv, scratch=[big, big],
    )
    near = jnp.concatenate([qg[TOKENS:], qgp[TOKENS:]], axis=0)
    qgs = tuple(shift(near, step) for step in (2, 4, 6))
    all_qg = exchange(packed, planes)
    (dq,) = call(
        grad_query_kernel, [((HALF, PAIR), BF)], 2, offsets, counts, qg, qg_top, st1, st, kv, kvp, ring_kv, all_kv,
        scratch=[(2, GROUP * ROWS1, LANES), big, big],
    )
    (level0,) = call(grad_key_kernel, [((TOKENS, PAIR), F32)], 1, counts, kv, qg, st, qgp)
    (early,) = call(
        level1_keys_kernel, [((TOKENS, PAIR), F32)], 2, offsets, counts, copies, near, *qgs, st1, level0,
        scratch=[(OWN, LANES)] * 2,
    )
    dk, dv = call(last_kernel, [((HALF, PAIR), BF)] * 2, 2, offsets, counts, copies, all_qg, early)
    return dq, dk, dv


def solution(mesh):
    split = P("seq", "head")
    return jax.shard_map(
        per_device,
        mesh=mesh,
        in_specs=(split, split, split, split, P("head", None), P(), P()),
        out_specs=(split, split, split),
        check_vma=False,
    )
```

```python
import math

import jax
import jax.numpy as jnp
from jax import lax
from jax.experimental import pallas as pl
from jax.experimental.pallas import tpu as pltpu
from jax.sharding import PartitionSpec as P

HEAD = 48
HEADS = 4
TOKENS = 256
HALF = TOKENS // 2
FEAT = HEADS * HEAD
PAIR = 2 * FEAT
LANES = 256
SIDE = 128
MID = 4
TOP = 16
GROUP = 8
ROWS1 = TOKENS // MID
ROWS2 = TOKENS // TOP
ROWS = ROWS1 + ROWS2
OWN = GROUP * ROWS1
TAIL = 2 * ROWS2 + 48
SCALE = HEAD**-0.5
ROOT = math.sqrt(HEAD)
EXP2 = SCALE * math.log2(math.e)
BIG = 1e30
VMEM_BYTES = 20 * 1024 * 1024
BF = jnp.bfloat16
F32 = jnp.float32

VMEM = pl.BlockSpec(memory_space=pltpu.VMEM)
SMEM = pl.BlockSpec(memory_space=pltpu.SMEM)


def iota(shape, dim):
    return lax.broadcasted_iota(jnp.int32, shape, dim)


def nt(a, b):
    return lax.dot_general(a, b, (((1,), (1,)), ((), ())), preferred_element_type=F32)


def nn(a, b):
    return jnp.dot(a, b, preferred_element_type=F32)


def first_mask(h, shape):
    lane = iota(shape, 1)
    return ((lane >= HEAD * h) & (lane < HEAD * (h + 1))) | ((lane >= FEAT + 8 * h) & (lane < FEAT + 8 * h + 8))


def second_mask(h, shape):
    lane = iota(shape, 1)
    at = lane - (LANES - FEAT)
    return ((at >= HEAD * h) & (at < HEAD * (h + 1))) | ((lane >= 8 * h) & (lane < 8 * h + 8))


def helper_mask(h, shape):
    lane = iota(shape, 1) & 63
    return (lane >= 8 * h) & (lane < 8 * h + 8)


def first_view(pair, helpers):
    left, right = pair[:, :SIDE], pair[:, SIDE:LANES]
    return jnp.concatenate([left, jnp.where(iota(right.shape, 1) < 64, right, helpers)], axis=1)


def second_view(pair, helpers):
    left, right = pair[:, SIDE:LANES], pair[:, LANES:]
    return jnp.concatenate([jnp.where(iota(left.shape, 1) < 64, helpers, left), right], axis=1)


def query_helpers(rows):
    lane = iota((rows, SIDE), 1)
    return jnp.where((lane >= 64) & (lane < 96) & ((lane & 7) == 3), 1.0, 0.0).astype(BF)


def key_helpers(mask):
    lane = iota(mask.shape, 1)
    slot = lane & 7
    used = (lane & 63) < 32
    value = jnp.where(slot < 3, -1.0, jnp.where(slot == 3, mask, jnp.where(slot < 7, -1.0, 0.0)))
    value = jnp.where((lane < 64) & (slot < 4), 0.0, value)
    value = jnp.where((lane >= 64) & (slot >= 4), 0.0, value)
    return jnp.where(used, value, 0.0).astype(BF)


def lane_offsets(offsets, level, shape):
    h = (iota(shape, 1) >> 3) & 3
    base = lax.axis_index("head") * HEADS
    at = [offsets[level, base + i] for i in range(HEADS)]
    return jnp.where(h == 0, at[0], jnp.where(h == 1, at[1], jnp.where(h == 2, at[2], at[3])))


def dilated_mask(offsets, level, count):
    rows, rate = (ROWS1, MID) if level == 0 else (ROWS2, TOP)
    shape = (rows, SIDE)
    return jnp.where(rate * iota(shape, 0) + lane_offsets(offsets, level, shape) < count, 0.0, -BIG)


def positions(shape):
    row = iota(shape, 0)
    return jnp.where(row < HALF, 2 * row, 2 * (row - HALF) + 1)


def full_mask(count):
    return jnp.where(positions((TOKENS, SIDE)) < count, 0.0, -BIG)


def by_parity(paired):
    halves = [
        jnp.concatenate([paired[:, (2 * h + t) * HEAD : (2 * h + t + 1) * HEAD] for h in range(HEADS)], axis=1)
        for t in range(2)
    ]
    return jnp.concatenate(halves, axis=0)


def to_paired(flat):
    flat = flat.astype(BF)
    pieces = []
    for h in range(HEADS):
        for t in range(2):
            pieces.append(flat[t * HALF : (t + 1) * HALF, h * HEAD : (h + 1) * HEAD])
    return jnp.concatenate(pieces, axis=1)


def place_of(offsets, level, h, shape, dim):
    rate = MID if level == 0 else TOP
    return rate * iota(shape, dim) + offsets[level, lax.axis_index("head") * HEADS + h]


def chosen(offsets, level, h, shape, dim):
    place = place_of(offsets, level, h, shape, dim)
    return ((place >> 1) + (place & 1) * HALF) == iota(shape, 1 - dim)


def select_stack(offsets, level):
    rows = ROWS1 if level == 0 else ROWS2
    return jnp.concatenate(
        [jnp.where(chosen(offsets, level, h, (rows, TOKENS), 0), 1.0, 0.0) for h in range(HEADS)], axis=0
    ).astype(BF)


def folded(stack, rows, mask):
    total = None
    for h in range(HEADS):
        part = jnp.where(mask(h, (rows, stack.shape[1])), stack[h * rows : (h + 1) * rows], 0.0)
        total = part if total is None else total + part
    return total


def head_stack(rows, mask):
    return jnp.concatenate([rows * mask(h, (1, rows.shape[1])).astype(BF) for h in range(HEADS)], axis=0)


def feature_mask(h, shape):
    lane = iota(shape, 1)
    return (lane >= HEAD * h) & (lane < HEAD * (h + 1))


def split3(x):
    high = x.astype(BF)
    rest = x - high.astype(F32)
    mid = rest.astype(BF)
    low = (rest - mid.astype(F32)).astype(BF)
    return high, mid, low


def paired_rows(offsets, source):
    parts = []
    for level, rows in ((0, ROWS1), (1, ROWS2)):
        total = None
        for h in range(HEADS):
            row = place_of(offsets, level, h, (rows, HALF), 0) >> 1
            pick = jnp.where(row == iota((rows, HALF), 1), 1.0, 0.0).astype(BF)
            both = nn(pick, source[:, 2 * HEAD * h : 2 * HEAD * (h + 1)])
            odd = (place_of(offsets, level, h, (rows, HEAD), 0) & 1) == 1
            part = jnp.where(odd, both[:, HEAD:], both[:, :HEAD])
            total = [part] if total is None else total + [part]
        parts.append(jnp.concatenate(total, axis=1))
    return jnp.concatenate(parts, axis=0)


def rows_kernel(offsets, k, v, own, copies):
    both = jnp.concatenate([paired_rows(offsets, k), paired_rows(offsets, v)], axis=1).astype(BF)
    own[...] = both
    for i in range(GROUP):
        copies[i] = both


def pairs_kernel(k, v, k_next, v_next, kv, kv_next):
    for a, b, out in ((k, v, kv), (k_next, v_next, kv_next)):
        out[...] = jnp.concatenate([by_parity(a[...]), by_parity(b[...])], axis=1)


def repeat_kernel(rows, out):
    block = rows[:, ROWS1:].reshape(GROUP * ROWS2, PAIR)
    for i in range(GROUP):
        out[i] = block


def proj_kernel(offsets, counts, gy, w, q, qg, qg_top):
    total = jnp.zeros((TOKENS, FEAT), F32)
    for i in range(4):
        flat = by_parity(gy[i])
        total = total + nt(flat, w[:, i * FEAT : (i + 1) * FEAT])
    total = jnp.where(positions((TOKENS, FEAT)) < counts[lax.axis_index("seq")], total, 0.0)
    flat = jnp.concatenate([by_parity(q[...]), total.astype(BF)], axis=1)
    qg[:TOKENS] = flat

    def mask(h, shape):
        return feature_mask(h, shape) | feature_mask(h + HEADS, shape)

    qg[TOKENS : TOKENS + ROWS1] = folded(nn(select_stack(offsets, 0), flat), ROWS1, mask).astype(BF)
    qg_top[...] = folded(nn(select_stack(offsets, 1), flat), ROWS2, mask).astype(BF)


def level_stats(keys, values, queries, grads):
    scores = [nt(k, queries) for k in keys]
    top = scores[0].max(axis=0, keepdims=True)
    for s in scores[1:]:
        top = jnp.maximum(top, s.max(axis=0, keepdims=True))
    mass = dot = None
    for s, v in zip(scores, values):
        e = jnp.exp2((s - top) * EXP2)
        part = e.sum(axis=0, keepdims=True)
        part_dot = (e * nt(v, grads)).sum(axis=0, keepdims=True)
        mass = part if mass is None else mass + part
        dot = part_dot if dot is None else dot + part_dot
    return top, mass, dot


def spread(stats, stack, rows):
    top, mass, dot = stats
    width = top.shape[1]
    lane = iota((HEADS, width), 1)
    row = iota((HEADS, width), 0)
    own = (lane >= rows * row) & (lane < rows * (row + 1))
    placed = [jnp.where(own, x, 0.0) for x in (top, mass, dot, jnp.ones_like(top))]
    placed = jnp.concatenate(placed, axis=0)
    out = sum(nn(term, stack) for term in split3(placed))
    there = out[12:16] > 0.5
    return jnp.where(there, out[0:4], -BIG), out[4:8], out[8:12]


def merged(parts):
    top = parts[0][0]
    for p in parts[1:]:
        top = jnp.maximum(top, p[0])
    mass = dot = 0.0
    for p in parts:
        f = jnp.exp2((p[0] - top) * EXP2)
        mass = mass + p[1] * f
        dot = dot + p[2] * f
    return top, mass, dot


def fill_level1(offsets, counts, rows, kv1):
    seq = lax.axis_index("seq")
    base = seq - (seq & (GROUP - 1))
    for s in range(GROUP):
        helpers = key_helpers(dilated_mask(offsets, 0, counts[base + s]))
        block = rows[s, :ROWS1]
        kv1[0, s * ROWS1 : (s + 1) * ROWS1] = first_view(block, helpers)
        kv1[1, s * ROWS1 : (s + 1) * ROWS1] = second_view(block, helpers)


def by_head(x, width):
    return jnp.concatenate([x[:, h * width : (h + 1) * width] for h in range(HEADS)], axis=0)


def level0_kernel(counts, qg, kv, kvp, stats):
    seq = lax.axis_index("seq")
    flat = qg[:TOKENS]
    queries = head_stack(first_view(flat, query_helpers(TOKENS)), first_mask)
    grads = head_stack(second_view(flat, jnp.zeros((TOKENS, SIDE), BF)), second_mask)
    own = key_helpers(full_mask(counts[seq]))
    other = key_helpers(full_mask(counts[seq ^ 1]))
    keys = (first_view(kv[...], own), first_view(kvp[...], other))
    values = (second_view(kv[...], own), second_view(kvp[...], other))
    for i, x in enumerate(level_stats(keys, values, queries, grads)):
        stats[4 * i : 4 * i + 4] = by_head(x, TOKENS)
    stats[12:16] = jnp.zeros((4, TOKENS), F32)


def level1_kernel(offsets, counts, qg, qg_top, rows, stats, tail, kv1):
    fill_level1(offsets, counts, rows, kv1)
    level0 = (stats[0:4], stats[4:8], stats[8:12])
    block = qg[TOKENS : TOKENS + ROWS1]
    q1 = head_stack(first_view(block, query_helpers(ROWS1)), first_mask)
    g1 = head_stack(second_view(block, jnp.zeros((ROWS1, SIDE), BF)), second_mask)
    select1, select2 = select_stack(offsets, 0), select_stack(offsets, 1)
    level1 = spread(level_stats((kv1[0],), (kv1[1],), q1, g1), select1, ROWS1)
    terms = split3(jnp.concatenate(merged((level0, level1)), axis=0))
    own_head = [(iota((3 * HEADS, 1), 0) & 3) == h for h in range(HEADS)]
    empty = jnp.zeros((3 * HEADS, SIDE - ROWS), F32)
    chosen_terms = []
    for term in terms:
        one, two = nt(term, select1), nt(term, select2)
        row1 = row2 = 0.0
        for h in range(HEADS):
            row1 = row1 + jnp.where(own_head[h], one[:, h * ROWS1 : (h + 1) * ROWS1], 0.0)
            row2 = row2 + jnp.where(own_head[h], two[:, h * ROWS2 : (h + 1) * ROWS2], 0.0)
        chosen_terms.append(jnp.concatenate([row1, row2, empty], axis=1))
    pad = jnp.zeros((16 - 3 * HEADS, PAIR), F32)
    tail[:ROWS2] = qg_top[...]
    tail[ROWS2 : 2 * ROWS2] = jnp.concatenate([jnp.concatenate(chosen_terms, axis=1), pad], axis=0).astype(BF)
    for i, term in enumerate(terms):
        wide = jnp.concatenate([term.astype(F32), jnp.zeros((3 * HEADS, PAIR - LANES), F32)], axis=1)
        tail[16 * (i + 2) : 16 * (i + 3)] = jnp.concatenate([wide, pad], axis=0).astype(BF)


def fill_level2(offsets, counts, rows, keys, values):
    for a in range(GROUP):
        for s in range(GROUP):
            helpers = key_helpers(dilated_mask(offsets, 1, counts[a * GROUP + s]))
            block = rows[a, s * ROWS2 : (s + 1) * ROWS2]
            at = (a * GROUP + s) * ROWS2
            keys[at : at + ROWS2] = first_view(block, helpers)
            values[at : at + ROWS2] = second_view(block, helpers)


def summed_terms(ref, at):
    wide = ref[at : at + 16].astype(F32)
    return wide[:, :SIDE] + wide[:, SIDE : 2 * SIDE] + wide[:, 2 * SIDE :]


def finish_kernel(offsets, counts, tails, rows, st1, st, packed, keys, values):
    fill_level2(offsets, counts, rows, keys, values)
    starts = [0, TAIL] + [2 * TAIL + 2 * ROWS2 * i for i in range(GROUP - 2)]
    block = jnp.concatenate([tails[at : at + ROWS2] for at in starts], axis=0)
    width = GROUP * ROWS2
    q2 = head_stack(first_view(block, query_helpers(width)), first_mask)
    g2 = head_stack(second_view(block, jnp.zeros((width, SIDE), BF)), second_mask)
    flat = level_stats((keys[...],), (values[...],), q2, g2)
    level2 = [by_head(x, width) for x in flat]
    small = [summed_terms(tails, at + ROWS2) for at in starts]
    early1 = jnp.concatenate([x[:, :ROWS1] for x in small], axis=1)
    early2 = jnp.concatenate([x[:, ROWS1:ROWS] for x in small], axis=1)
    early0 = [
        sum(tails[at + 16 * i : at + 16 * (i + 1), :LANES].astype(F32) for i in range(2, 5)) for at in (0, TAIL)
    ]
    early = jnp.concatenate([early1, *early0], axis=1)
    total_rows = GROUP * ROWS1 + 2 * TOKENS
    shape = (width, total_rows)
    lane = iota(shape, 1)
    row = iota(shape, 0)
    ring = lane < GROUP * ROWS1
    inside = (lane - GROUP * ROWS1) & (TOKENS - 1)
    where0 = jnp.where(inside < HALF, 2 * inside, 2 * (inside - HALF) + 1)
    shard = jnp.where(ring, lane >> 6, (lane - GROUP * ROWS1) >> 8)
    same = shard == (row >> 4)
    head = lax.axis_index("head") * HEADS
    spread2 = []
    for h in range(HEADS):
        place = jnp.where(ring, MID * (lane & (ROWS1 - 1)) + offsets[0, head + h], where0)
        hit = same & (place == TOP * (row & (ROWS2 - 1)) + offsets[1, head + h])
        one_hot = jnp.where(hit, 1.0, 0.0).astype(BF)
        values_h = jnp.concatenate([x[h : h + 1] for x in level2] + [jnp.ones((1, width), F32)], axis=0)
        spread2.append(sum(nn(term, one_hot) for term in split3(values_h)))
    late = [jnp.concatenate([x[i : i + 1] for x in spread2], axis=0) for i in range(4)]
    late[0] = jnp.where(late[3] > 0.5, late[0], -BIG)
    first = merged(((early[0:4], early[4:8], early[8:12]), late[:3]))
    second = merged(((early2[0:4], early2[4:8], early2[8:12]), level2))
    top, total, dot = (jnp.concatenate([x, y], axis=1) for x, y in zip(first, second))
    grad_dot = dot / total
    log_total = top + jnp.log(total) * ROOT
    count = total_rows + width
    columns = jnp.concatenate(
        [x.astype(F32) for x in (*split3(log_total), *split3(grad_dot))]
        + [jnp.ones((HEADS, count), F32), jnp.zeros((HEADS, count), F32)],
        axis=0,
    )
    at = iota((8 * HEADS, SIDE), 0)
    s, h = at >> 2, at & 3
    slot = jnp.where(s < 3, s, jnp.where(s < 6, s + 1, jnp.where(s == 6, 3, 7)))
    place = jnp.where((iota((8 * HEADS, SIDE), 1) & 63) == 8 * h + slot, 1.0, 0.0).astype(BF)
    full = nn(columns.T.astype(BF), place).astype(BF)
    st1[...] = full[:OWN]
    st[...] = full[OWN:]
    wide = jnp.concatenate([block, full[total_rows:]], axis=1)
    for n in range(GROUP):
        packed[n] = wide


def scatter_rows(offsets, parts1, parts2, shift):
    def mask(h, shape):
        lane = iota(shape, 1) - shift
        return (lane >= HEAD * h) & (lane < HEAD * (h + 1))

    total = None
    for level, part, rows in ((0, parts1, ROWS1), (1, parts2, ROWS2)):
        if part is None:
            continue
        place = jnp.concatenate(
            [jnp.where(chosen(offsets, level, h, (TOKENS, rows), 1), 1.0, 0.0) for h in range(HEADS)], axis=1
        ).astype(BF)
        part = jnp.concatenate(
            [jnp.where(mask(h, (rows, LANES)), part[h * rows : (h + 1) * rows], 0.0) for h in range(HEADS)], axis=0
        )
        high = part.astype(BF)
        low = (part - high.astype(F32)).astype(BF)
        got = nn(place, high) + nn(place, low)
        total = got if total is None else total + got
    return total


def grad_query_kernel(offsets, counts, qg, qg_top, st1, st, kv, kvp, rows1, rows2, dq, kv1, keys2, values2):
    seq = lax.axis_index("seq")
    fill_level1(offsets, counts, rows1, kv1)
    fill_level2(offsets, counts, rows2, keys2, values2)
    own = key_helpers(full_mask(counts[seq]))
    other = key_helpers(full_mask(counts[seq ^ 1]))
    keys = (first_view(kv[...], own), first_view(kvp[...], other))
    values = (second_view(kv[...], own), second_view(kvp[...], other))

    def back(queries, grads, keys, values):
        total = None
        for kk, vv in zip(keys, values):
            weight = jnp.exp2(nt(queries, kk) * EXP2)
            score = (weight * nt(grads, vv)).astype(BF)
            part = nn(score, kk)
            total = part if total is None else total + part
        return total

    flat = qg[:TOKENS]
    mine = st[:TOKENS]
    queries, grads = first_view(flat, mine), second_view(flat, mine)
    part = back(head_stack(queries, first_mask), head_stack(grads, second_mask), keys, values)
    total = folded(part, TOKENS, feature_mask)
    got = []
    for block, helpers, ks, vs in (
        (qg[TOKENS:], st1[:ROWS1], kv1[0], kv1[1]),
        (qg_top[...], st[2 * TOKENS : 2 * TOKENS + ROWS2], keys2[...], values2[...]),
    ):
        qs = head_stack(first_view(block, helpers), first_mask)
        gs = head_stack(second_view(block, helpers), second_mask)
        got.append(back(qs, gs, (ks,), (vs,)))
    total = (total + scatter_rows(offsets, got[0], got[1], 0)) * SCALE
    dq[...] = to_paired(total)


def key_back(keys, values, queries, grads):
    total_k = total_v = None
    for qq, gg in zip(queries, grads):
        weight = jnp.exp2(nt(keys, qq) * EXP2)
        score = (weight * nt(values, gg)).astype(BF)
        part_k = nn(score, qq)
        part_v = nn(weight.astype(BF), gg)
        total_k = part_k if total_k is None else total_k + part_k
        total_v = part_v if total_v is None else total_v + part_v
    return total_k, total_v


def grad_key_kernel(counts, kv, qg, st, qgp, out):
    own = key_helpers(full_mask(counts[lax.axis_index("seq")]))
    keys, values = first_view(kv[...], own), second_view(kv[...], own)
    flat, other = qg[:TOKENS], qgp[:TOKENS]
    mine, next_st = st[:TOKENS], st[TOKENS : 2 * TOKENS]
    queries = (first_view(flat, mine), first_view(other, next_st))
    grads = (second_view(flat, mine), second_view(other, next_st))
    part_k, part_v = key_back(head_stack(keys, first_mask), head_stack(values, second_mask), queries, grads)
    out[:, :FEAT] = folded(part_k, TOKENS, feature_mask)[:, :FEAT]
    out[:, FEAT:] = folded(part_v, TOKENS, second_mask)[:, LANES - FEAT :]


def level1_keys_kernel(offsets, counts, own, near, far2, far4, far6, st1, level0, out, qs, gs):
    for i in range(GROUP):
        block = (near, far2, far4, far6)[i // 2][(i & 1) * ROWS1 : (i & 1) * ROWS1 + ROWS1]
        helpers = st1[i * ROWS1 : (i + 1) * ROWS1]
        qs[i * ROWS1 : (i + 1) * ROWS1] = first_view(block, helpers)
        gs[i * ROWS1 : (i + 1) * ROWS1] = second_view(block, helpers)
    mine = key_helpers(dilated_mask(offsets, 0, counts[lax.axis_index("seq")]))
    block = own[:ROWS1]
    k1 = head_stack(first_view(block, mine), first_mask)
    v1 = head_stack(second_view(block, mine), second_mask)
    k1_part, v1_part = key_back(k1, v1, (qs[...],), (gs[...],))
    out[:, :FEAT] = level0[:, :FEAT] + scatter_rows(offsets, k1_part, None, 0)[:, :FEAT]
    out[:, FEAT:] = level0[:, FEAT:] + scatter_rows(offsets, v1_part, None, LANES - FEAT)[:, LANES - FEAT :]


def last_kernel(offsets, counts, own, all_qg, early, dk, dv):
    full = all_qg[...].reshape(GROUP * GROUP * ROWS2, PAIR + SIDE)
    helpers = full[:, PAIR:]
    queries, grads = first_view(full[:, :PAIR], helpers), second_view(full[:, :PAIR], helpers)
    mine = key_helpers(dilated_mask(offsets, 1, counts[lax.axis_index("seq")]))
    block = own[ROWS1:]
    k2 = head_stack(first_view(block, mine), first_mask)
    v2 = head_stack(second_view(block, mine), second_mask)
    k2_part, v2_part = key_back(k2, v2, (queries,), (grads,))
    dk[...] = to_paired((early[:, :FEAT] + scatter_rows(offsets, None, k2_part, 0)[:, :FEAT]) * SCALE)
    dv[...] = to_paired(early[:, FEAT:] + scatter_rows(offsets, None, v2_part, LANES - FEAT)[:, LANES - FEAT :])


def call(kernel, outs, n_smem, *args, scratch=()):
    return pl.pallas_call(
        kernel,
        out_shape=[jax.ShapeDtypeStruct(s, d) for s, d in outs],
        in_specs=[SMEM] * n_smem + [VMEM] * (len(args) - n_smem),
        out_specs=[VMEM] * len(outs),
        scratch_shapes=[pltpu.VMEM(s, BF) for s in scratch],
        compiler_params=pltpu.CompilerParams(vmem_limit_bytes=VMEM_BYTES),
    )(*args)


def per_device(queries, keys, values, grad_y, out_weight, counts, offsets):
    n_seq = lax.axis_size("seq")
    rings = [[GROUP * b + i for i in range(GROUP)] for b in range(n_seq // GROUP)]
    planes = [[GROUP * b + i for b in range(n_seq // GROUP)] for i in range(GROUP)]

    def swap(x, bits):
        return lax.ppermute(x, "seq", [(i, i ^ bits) for i in range(n_seq)])

    def shift(x, step):
        return lax.ppermute(x, "seq", [(r[i], r[(i + step) % GROUP]) for r in rings for i in range(GROUP)])

    def exchange(copies, groups):
        return lax.all_to_all(copies, "seq", 0, 0, axis_index_groups=groups)

    def far(own, near):
        both = jnp.concatenate([own, near], axis=0)
        return tuple(shift(both, step) for step in (2, 4, 6))

    k_next, v_next = swap(keys, 1), swap(values, 1)
    own, copies = call(
        rows_kernel, [((ROWS, PAIR), BF), ((GROUP, ROWS, PAIR), BF)], 1, offsets, keys, values
    )
    copies, k_next, v_next = lax.optimization_barrier((copies, k_next, v_next))
    ring_kv = exchange(copies, rings)
    flat = (TOKENS, PAIR)
    kv, kvp = call(pairs_kernel, [(flat, BF)] * 2, 0, keys, values, k_next, v_next)
    gy = lax.all_gather(grad_y, "head", axis=0)
    qg, qg_top = call(
        proj_kernel, [((TOKENS + ROWS1, PAIR), BF), ((ROWS2, PAIR), BF)], 2, offsets, counts, gy, out_weight, queries
    )
    qgp = swap(qg, 1)
    (stats,) = call(level0_kernel, [((16, TOKENS), F32)], 1, counts, qg, kv, kvp)
    ring_kv, stats = lax.optimization_barrier((ring_kv, stats))
    (tail,) = call(
        level1_kernel, [((TAIL, PAIR), BF)], 2, offsets, counts, qg, qg_top, ring_kv, stats,
        scratch=[(2, GROUP * ROWS1, LANES)],
    )
    tail_next = swap(tail, 1)
    (repeated,) = call(repeat_kernel, [((GROUP, GROUP * ROWS2, PAIR), BF)], 0, ring_kv)
    repeated, tail_next, qgp = lax.optimization_barrier((repeated, tail_next, qgp))
    all_kv = exchange(repeated, planes)
    tails = far(tail[: 2 * ROWS2], tail_next[: 2 * ROWS2])
    tails, qgp = lax.optimization_barrier((jnp.concatenate([tail, tail_next, *tails], axis=0), qgp))
    big = (GROUP * GROUP * ROWS2, LANES)
    st_rows = 2 * TOKENS + GROUP * ROWS2
    st1, st, packed = call(
        finish_kernel, [((OWN, SIDE), BF), ((st_rows, SIDE), BF), ((GROUP, GROUP * ROWS2, PAIR + SIDE), BF)], 2, offsets, counts,
        tails, all_kv, scratch=[big, big],
    )
    near = jnp.concatenate([qg[TOKENS:], qgp[TOKENS:]], axis=0)
    qgs = tuple(shift(near, step) for step in (2, 4, 6))
    all_qg = exchange(packed, planes)
    (dq,) = call(
        grad_query_kernel, [((HALF, PAIR), BF)], 2, offsets, counts, qg, qg_top, st1, st, kv, kvp, ring_kv, all_kv,
        scratch=[(2, GROUP * ROWS1, LANES), big, big],
    )
    (level0,) = call(grad_key_kernel, [((TOKENS, PAIR), F32)], 1, counts, kv, qg, st, qgp)
    (early,) = call(
        level1_keys_kernel, [((TOKENS, PAIR), F32)], 2, offsets, counts, own, near, *qgs, st1, level0,
        scratch=[(OWN, LANES)] * 2,
    )
    dk, dv = call(last_kernel, [((HALF, PAIR), BF)] * 2, 2, offsets, counts, own, all_qg, early)
    return dq, dk, dv


def solution(mesh):
    split = P("seq", "head")
    return jax.shard_map(
        per_device,
        mesh=mesh,
        in_specs=(split, split, split, split, P("head", None), P(), P()),
        out_specs=(split, split, split),
        check_vma=False,
    )
```

```python
import math

import jax
import jax.numpy as jnp
from jax import lax
from jax.experimental import pallas as pl
from jax.experimental.pallas import tpu as pltpu
from jax.sharding import PartitionSpec as P

HEAD = 48
HEADS = 4
TOKENS = 256
HALF = TOKENS // 2
FEAT = HEADS * HEAD
PAIR = 2 * FEAT
LANES = 256
SIDE = 128
MID = 4
TOP = 16
GROUP = 8
ROWS1 = TOKENS // MID
ROWS2 = TOKENS // TOP
ROWS = ROWS1 + ROWS2
OWN = GROUP * ROWS1
TAIL = 2 * ROWS2 + 48
SCALE = HEAD**-0.5
ROOT = math.sqrt(HEAD)
EXP2 = SCALE * math.log2(math.e)
BIG = 1e30
VMEM_BYTES = 20 * 1024 * 1024
BF = jnp.bfloat16
F32 = jnp.float32

VMEM = pl.BlockSpec(memory_space=pltpu.VMEM)
SMEM = pl.BlockSpec(memory_space=pltpu.SMEM)


def iota(shape, dim):
    return lax.broadcasted_iota(jnp.int32, shape, dim)


def nt(a, b):
    return lax.dot_general(a, b, (((1,), (1,)), ((), ())), preferred_element_type=F32)


def nn(a, b):
    return jnp.dot(a, b, preferred_element_type=F32)


def first_mask(h, shape):
    lane = iota(shape, 1)
    return ((lane >= HEAD * h) & (lane < HEAD * (h + 1))) | ((lane >= FEAT + 8 * h) & (lane < FEAT + 8 * h + 8))


def second_mask(h, shape):
    lane = iota(shape, 1)
    at = lane - (LANES - FEAT)
    return ((at >= HEAD * h) & (at < HEAD * (h + 1))) | ((lane >= 8 * h) & (lane < 8 * h + 8))


def helper_mask(h, shape):
    lane = iota(shape, 1) & 63
    return (lane >= 8 * h) & (lane < 8 * h + 8)


def first_view(pair, helpers):
    left, right = pair[:, :SIDE], pair[:, SIDE:LANES]
    return jnp.concatenate([left, jnp.where(iota(right.shape, 1) < 64, right, helpers)], axis=1)


def second_view(pair, helpers):
    left, right = pair[:, SIDE:LANES], pair[:, LANES:]
    return jnp.concatenate([jnp.where(iota(left.shape, 1) < 64, helpers, left), right], axis=1)


def query_helpers(rows):
    lane = iota((rows, SIDE), 1)
    return jnp.where((lane >= 64) & (lane < 96) & ((lane & 7) == 3), 1.0, 0.0).astype(BF)


def key_helpers(mask):
    lane = iota(mask.shape, 1)
    slot = lane & 7
    used = (lane & 63) < 32
    value = jnp.where(slot < 3, -1.0, jnp.where(slot == 3, mask, jnp.where(slot < 7, -1.0, 0.0)))
    value = jnp.where((lane < 64) & (slot < 4), 0.0, value)
    value = jnp.where((lane >= 64) & (slot >= 4), 0.0, value)
    return jnp.where(used, value, 0.0).astype(BF)


def lane_offsets(offsets, level, shape):
    h = (iota(shape, 1) >> 3) & 3
    base = lax.axis_index("head") * HEADS
    at = [offsets[level, base + i] for i in range(HEADS)]
    return jnp.where(h == 0, at[0], jnp.where(h == 1, at[1], jnp.where(h == 2, at[2], at[3])))


def dilated_mask(offsets, level, count):
    rows, rate = (ROWS1, MID) if level == 0 else (ROWS2, TOP)
    shape = (rows, SIDE)
    return jnp.where(rate * iota(shape, 0) + lane_offsets(offsets, level, shape) < count, 0.0, -BIG)


def positions(shape):
    row = iota(shape, 0)
    return jnp.where(row < HALF, 2 * row, 2 * (row - HALF) + 1)


def full_mask(count):
    return jnp.where(positions((TOKENS, SIDE)) < count, 0.0, -BIG)


def by_parity(paired):
    halves = [
        jnp.concatenate([paired[:, (2 * h + t) * HEAD : (2 * h + t + 1) * HEAD] for h in range(HEADS)], axis=1)
        for t in range(2)
    ]
    return jnp.concatenate(halves, axis=0)


def to_paired(flat):
    flat = flat.astype(BF)
    pieces = []
    for h in range(HEADS):
        for t in range(2):
            pieces.append(flat[t * HALF : (t + 1) * HALF, h * HEAD : (h + 1) * HEAD])
    return jnp.concatenate(pieces, axis=1)


def place_of(offsets, level, h, shape, dim):
    rate = MID if level == 0 else TOP
    return rate * iota(shape, dim) + offsets[level, lax.axis_index("head") * HEADS + h]


def chosen(offsets, level, h, shape, dim):
    place = place_of(offsets, level, h, shape, dim)
    return ((place >> 1) + (place & 1) * HALF) == iota(shape, 1 - dim)


def select_stack(offsets, level):
    rows = ROWS1 if level == 0 else ROWS2
    return jnp.concatenate(
        [jnp.where(chosen(offsets, level, h, (rows, TOKENS), 0), 1.0, 0.0) for h in range(HEADS)], axis=0
    ).astype(BF)


def folded(stack, rows, mask):
    total = None
    for h in range(HEADS):
        part = jnp.where(mask(h, (rows, stack.shape[1])), stack[h * rows : (h + 1) * rows], 0.0)
        total = part if total is None else total + part
    return total


def head_stack(rows, mask):
    return jnp.concatenate([rows * mask(h, (1, rows.shape[1])).astype(BF) for h in range(HEADS)], axis=0)


def feature_mask(h, shape):
    lane = iota(shape, 1)
    return (lane >= HEAD * h) & (lane < HEAD * (h + 1))


def split3(x):
    high = x.astype(BF)
    rest = x - high.astype(F32)
    mid = rest.astype(BF)
    low = (rest - mid.astype(F32)).astype(BF)
    return high, mid, low


def paired_rows(offsets, source):
    parts = []
    for level, rows in ((0, ROWS1), (1, ROWS2)):
        total = None
        for h in range(HEADS):
            row = place_of(offsets, level, h, (rows, HALF), 0) >> 1
            pick = jnp.where(row == iota((rows, HALF), 1), 1.0, 0.0).astype(BF)
            both = nn(pick, source[:, 2 * HEAD * h : 2 * HEAD * (h + 1)])
            odd = (place_of(offsets, level, h, (rows, HEAD), 0) & 1) == 1
            part = jnp.where(odd, both[:, HEAD:], both[:, :HEAD])
            total = [part] if total is None else total + [part]
        parts.append(jnp.concatenate(total, axis=1))
    return jnp.concatenate(parts, axis=0)


def rows_kernel(offsets_far, k_far, v_far, own, copies, offsets, k, v, *semaphores):
    moves = [
        pltpu.make_async_copy(*x) for x in zip((offsets_far, k_far, v_far), (offsets, k, v), semaphores)
    ]
    for m in moves:
        m.start()
    for m in moves:
        m.wait()
    both = jnp.concatenate([paired_rows(offsets, k), paired_rows(offsets, v)], axis=1).astype(BF)
    own[...] = both
    for i in range(GROUP):
        copies[i] = both


def pairs_kernel(k, v, k_next, v_next, kv, kv_next):
    for a, b, out in ((k, v, kv), (k_next, v_next, kv_next)):
        out[...] = jnp.concatenate([by_parity(a[...]), by_parity(b[...])], axis=1)


def repeat_kernel(rows, out):
    block = rows[:, ROWS1:].reshape(GROUP * ROWS2, PAIR)
    for i in range(GROUP):
        out[i] = block


def proj_kernel(offsets, counts, gy, w, q, qg, qg_top):
    total = jnp.zeros((TOKENS, FEAT), F32)
    for i in range(4):
        flat = by_parity(gy[i])
        total = total + nt(flat, w[:, i * FEAT : (i + 1) * FEAT])
    total = jnp.where(positions((TOKENS, FEAT)) < counts[lax.axis_index("seq")], total, 0.0)
    flat = jnp.concatenate([by_parity(q[...]), total.astype(BF)], axis=1)
    qg[:TOKENS] = flat

    def mask(h, shape):
        return feature_mask(h, shape) | feature_mask(h + HEADS, shape)

    qg[TOKENS : TOKENS + ROWS1] = folded(nn(select_stack(offsets, 0), flat), ROWS1, mask).astype(BF)
    qg_top[...] = folded(nn(select_stack(offsets, 1), flat), ROWS2, mask).astype(BF)


def level_stats(keys, values, queries, grads):
    scores = [nt(k, queries) for k in keys]
    top = scores[0].max(axis=0, keepdims=True)
    for s in scores[1:]:
        top = jnp.maximum(top, s.max(axis=0, keepdims=True))
    mass = dot = None
    for s, v in zip(scores, values):
        e = jnp.exp2((s - top) * EXP2)
        part = e.sum(axis=0, keepdims=True)
        part_dot = (e * nt(v, grads)).sum(axis=0, keepdims=True)
        mass = part if mass is None else mass + part
        dot = part_dot if dot is None else dot + part_dot
    return top, mass, dot


def spread(stats, stack, rows):
    top, mass, dot = stats
    width = top.shape[1]
    lane = iota((HEADS, width), 1)
    row = iota((HEADS, width), 0)
    own = (lane >= rows * row) & (lane < rows * (row + 1))
    placed = [jnp.where(own, x, 0.0) for x in (top, mass, dot, jnp.ones_like(top))]
    placed = jnp.concatenate(placed, axis=0)
    out = sum(nn(term, stack) for term in split3(placed))
    there = out[12:16] > 0.5
    return jnp.where(there, out[0:4], -BIG), out[4:8], out[8:12]


def merged(parts):
    top = parts[0][0]
    for p in parts[1:]:
        top = jnp.maximum(top, p[0])
    mass = dot = 0.0
    for p in parts:
        f = jnp.exp2((p[0] - top) * EXP2)
        mass = mass + p[1] * f
        dot = dot + p[2] * f
    return top, mass, dot


def fill_level1(offsets, counts, rows, kv1):
    seq = lax.axis_index("seq")
    base = seq - (seq & (GROUP - 1))
    for s in range(GROUP):
        helpers = key_helpers(dilated_mask(offsets, 0, counts[base + s]))
        block = rows[s, :ROWS1]
        kv1[0, s * ROWS1 : (s + 1) * ROWS1] = first_view(block, helpers)
        kv1[1, s * ROWS1 : (s + 1) * ROWS1] = second_view(block, helpers)


def by_head(x, width):
    return jnp.concatenate([x[:, h * width : (h + 1) * width] for h in range(HEADS)], axis=0)


def level0_kernel(counts, qg, kv, kvp, stats):
    seq = lax.axis_index("seq")
    flat = qg[:TOKENS]
    queries = head_stack(first_view(flat, query_helpers(TOKENS)), first_mask)
    grads = head_stack(second_view(flat, jnp.zeros((TOKENS, SIDE), BF)), second_mask)
    own = key_helpers(full_mask(counts[seq]))
    other = key_helpers(full_mask(counts[seq ^ 1]))
    keys = (first_view(kv[...], own), first_view(kvp[...], other))
    values = (second_view(kv[...], own), second_view(kvp[...], other))
    for i, x in enumerate(level_stats(keys, values, queries, grads)):
        stats[4 * i : 4 * i + 4] = by_head(x, TOKENS)
    stats[12:16] = jnp.zeros((4, TOKENS), F32)


def level1_kernel(offsets, counts, qg, qg_top, rows, stats, tail, kv1):
    fill_level1(offsets, counts, rows, kv1)
    level0 = (stats[0:4], stats[4:8], stats[8:12])
    block = qg[TOKENS : TOKENS + ROWS1]
    q1 = head_stack(first_view(block, query_helpers(ROWS1)), first_mask)
    g1 = head_stack(second_view(block, jnp.zeros((ROWS1, SIDE), BF)), second_mask)
    select1, select2 = select_stack(offsets, 0), select_stack(offsets, 1)
    level1 = spread(level_stats((kv1[0],), (kv1[1],), q1, g1), select1, ROWS1)
    terms = split3(jnp.concatenate(merged((level0, level1)), axis=0))
    own_head = [(iota((3 * HEADS, 1), 0) & 3) == h for h in range(HEADS)]
    empty = jnp.zeros((3 * HEADS, SIDE - ROWS), F32)
    chosen_terms = []
    for term in terms:
        one, two = nt(term, select1), nt(term, select2)
        row1 = row2 = 0.0
        for h in range(HEADS):
            row1 = row1 + jnp.where(own_head[h], one[:, h * ROWS1 : (h + 1) * ROWS1], 0.0)
            row2 = row2 + jnp.where(own_head[h], two[:, h * ROWS2 : (h + 1) * ROWS2], 0.0)
        chosen_terms.append(jnp.concatenate([row1, row2, empty], axis=1))
    pad = jnp.zeros((16 - 3 * HEADS, PAIR), F32)
    tail[:ROWS2] = qg_top[...]
    tail[ROWS2 : 2 * ROWS2] = jnp.concatenate([jnp.concatenate(chosen_terms, axis=1), pad], axis=0).astype(BF)
    for i, term in enumerate(terms):
        wide = jnp.concatenate([term.astype(F32), jnp.zeros((3 * HEADS, PAIR - LANES), F32)], axis=1)
        tail[16 * (i + 2) : 16 * (i + 3)] = jnp.concatenate([wide, pad], axis=0).astype(BF)


def fill_level2(offsets, counts, rows, keys, values):
    for a in range(GROUP):
        for s in range(GROUP):
            helpers = key_helpers(dilated_mask(offsets, 1, counts[a * GROUP + s]))
            block = rows[a, s * ROWS2 : (s + 1) * ROWS2]
            at = (a * GROUP + s) * ROWS2
            keys[at : at + ROWS2] = first_view(block, helpers)
            values[at : at + ROWS2] = second_view(block, helpers)


def summed_terms(ref, at):
    wide = ref[at : at + 16].astype(F32)
    return wide[:, :SIDE] + wide[:, SIDE : 2 * SIDE] + wide[:, 2 * SIDE :]


def finish_kernel(offsets, counts, tails, rows, st1, st, packed, keys, values):
    fill_level2(offsets, counts, rows, keys, values)
    starts = [0, TAIL] + [2 * TAIL + 2 * ROWS2 * i for i in range(GROUP - 2)]
    block = jnp.concatenate([tails[at : at + ROWS2] for at in starts], axis=0)
    width = GROUP * ROWS2
    q2 = head_stack(first_view(block, query_helpers(width)), first_mask)
    g2 = head_stack(second_view(block, jnp.zeros((width, SIDE), BF)), second_mask)
    flat = level_stats((keys[...],), (values[...],), q2, g2)
    level2 = [by_head(x, width) for x in flat]
    small = [summed_terms(tails, at + ROWS2) for at in starts]
    early1 = jnp.concatenate([x[:, :ROWS1] for x in small], axis=1)
    early2 = jnp.concatenate([x[:, ROWS1:ROWS] for x in small], axis=1)
    early0 = [
        sum(tails[at + 16 * i : at + 16 * (i + 1), :LANES].astype(F32) for i in range(2, 5)) for at in (0, TAIL)
    ]
    early = jnp.concatenate([early1, *early0], axis=1)
    total_rows = GROUP * ROWS1 + 2 * TOKENS
    shape = (width, total_rows)
    lane = iota(shape, 1)
    row = iota(shape, 0)
    ring = lane < GROUP * ROWS1
    inside = (lane - GROUP * ROWS1) & (TOKENS - 1)
    where0 = jnp.where(inside < HALF, 2 * inside, 2 * (inside - HALF) + 1)
    shard = jnp.where(ring, lane >> 6, (lane - GROUP * ROWS1) >> 8)
    same = shard == (row >> 4)
    head = lax.axis_index("head") * HEADS
    spread2 = []
    for h in range(HEADS):
        place = jnp.where(ring, MID * (lane & (ROWS1 - 1)) + offsets[0, head + h], where0)
        hit = same & (place == TOP * (row & (ROWS2 - 1)) + offsets[1, head + h])
        one_hot = jnp.where(hit, 1.0, 0.0).astype(BF)
        values_h = jnp.concatenate([x[h : h + 1] for x in level2] + [jnp.ones((1, width), F32)], axis=0)
        spread2.append(sum(nn(term, one_hot) for term in split3(values_h)))
    late = [jnp.concatenate([x[i : i + 1] for x in spread2], axis=0) for i in range(4)]
    late[0] = jnp.where(late[3] > 0.5, late[0], -BIG)
    first = merged(((early[0:4], early[4:8], early[8:12]), late[:3]))
    second = merged(((early2[0:4], early2[4:8], early2[8:12]), level2))
    top, total, dot = (jnp.concatenate([x, y], axis=1) for x, y in zip(first, second))
    grad_dot = dot / total
    log_total = top + jnp.log(total) * ROOT
    count = total_rows + width
    columns = jnp.concatenate(
        [x.astype(F32) for x in (*split3(log_total), *split3(grad_dot))]
        + [jnp.ones((HEADS, count), F32), jnp.zeros((HEADS, count), F32)],
        axis=0,
    )
    at = iota((8 * HEADS, SIDE), 0)
    s, h = at >> 2, at & 3
    slot = jnp.where(s < 3, s, jnp.where(s < 6, s + 1, jnp.where(s == 6, 3, 7)))
    place = jnp.where((iota((8 * HEADS, SIDE), 1) & 63) == 8 * h + slot, 1.0, 0.0).astype(BF)
    full = nn(columns.T.astype(BF), place).astype(BF)
    st1[...] = full[:OWN]
    st[...] = full[OWN:]
    wide = jnp.concatenate([block, full[total_rows:]], axis=1)
    for n in range(GROUP):
        packed[n] = wide


def scatter_rows(offsets, parts1, parts2, shift):
    def mask(h, shape):
        lane = iota(shape, 1) - shift
        return (lane >= HEAD * h) & (lane < HEAD * (h + 1))

    total = None
    for level, part, rows in ((0, parts1, ROWS1), (1, parts2, ROWS2)):
        if part is None:
            continue
        place = jnp.concatenate(
            [jnp.where(chosen(offsets, level, h, (TOKENS, rows), 1), 1.0, 0.0) for h in range(HEADS)], axis=1
        ).astype(BF)
        part = jnp.concatenate(
            [jnp.where(mask(h, (rows, LANES)), part[h * rows : (h + 1) * rows], 0.0) for h in range(HEADS)], axis=0
        )
        high = part.astype(BF)
        low = (part - high.astype(F32)).astype(BF)
        got = nn(place, high) + nn(place, low)
        total = got if total is None else total + got
    return total


def grad_query_kernel(offsets, counts, qg, qg_top, st1, st, kv, kvp, rows1, rows2, dq, kv1, keys2, values2):
    seq = lax.axis_index("seq")
    fill_level1(offsets, counts, rows1, kv1)
    fill_level2(offsets, counts, rows2, keys2, values2)
    own = key_helpers(full_mask(counts[seq]))
    other = key_helpers(full_mask(counts[seq ^ 1]))
    keys = (first_view(kv[...], own), first_view(kvp[...], other))
    values = (second_view(kv[...], own), second_view(kvp[...], other))

    def back(queries, grads, keys, values):
        total = None
        for kk, vv in zip(keys, values):
            weight = jnp.exp2(nt(queries, kk) * EXP2)
            score = (weight * nt(grads, vv)).astype(BF)
            part = nn(score, kk)
            total = part if total is None else total + part
        return total

    flat = qg[:TOKENS]
    mine = st[:TOKENS]
    queries, grads = first_view(flat, mine), second_view(flat, mine)
    part = back(head_stack(queries, first_mask), head_stack(grads, second_mask), keys, values)
    total = folded(part, TOKENS, feature_mask)
    got = []
    for block, helpers, ks, vs in (
        (qg[TOKENS:], st1[:ROWS1], kv1[0], kv1[1]),
        (qg_top[...], st[2 * TOKENS : 2 * TOKENS + ROWS2], keys2[...], values2[...]),
    ):
        qs = head_stack(first_view(block, helpers), first_mask)
        gs = head_stack(second_view(block, helpers), second_mask)
        got.append(back(qs, gs, (ks,), (vs,)))
    total = (total + scatter_rows(offsets, got[0], got[1], 0)) * SCALE
    dq[...] = to_paired(total)


def key_back(keys, values, queries, grads):
    total_k = total_v = None
    for qq, gg in zip(queries, grads):
        weight = jnp.exp2(nt(keys, qq) * EXP2)
        score = (weight * nt(values, gg)).astype(BF)
        part_k = nn(score, qq)
        part_v = nn(weight.astype(BF), gg)
        total_k = part_k if total_k is None else total_k + part_k
        total_v = part_v if total_v is None else total_v + part_v
    return total_k, total_v


def grad_key_kernel(counts, kv, qg, st, qgp, out):
    own = key_helpers(full_mask(counts[lax.axis_index("seq")]))
    keys, values = first_view(kv[...], own), second_view(kv[...], own)
    flat, other = qg[:TOKENS], qgp[:TOKENS]
    mine, next_st = st[:TOKENS], st[TOKENS : 2 * TOKENS]
    queries = (first_view(flat, mine), first_view(other, next_st))
    grads = (second_view(flat, mine), second_view(other, next_st))
    part_k, part_v = key_back(head_stack(keys, first_mask), head_stack(values, second_mask), queries, grads)
    out[:, :FEAT] = folded(part_k, TOKENS, feature_mask)[:, :FEAT]
    out[:, FEAT:] = folded(part_v, TOKENS, second_mask)[:, LANES - FEAT :]


def level1_keys_kernel(offsets, counts, own, near, far2, far4, far6, st1, level0, out, qs, gs):
    for i in range(GROUP):
        block = (near, far2, far4, far6)[i // 2][(i & 1) * ROWS1 : (i & 1) * ROWS1 + ROWS1]
        helpers = st1[i * ROWS1 : (i + 1) * ROWS1]
        qs[i * ROWS1 : (i + 1) * ROWS1] = first_view(block, helpers)
        gs[i * ROWS1 : (i + 1) * ROWS1] = second_view(block, helpers)
    mine = key_helpers(dilated_mask(offsets, 0, counts[lax.axis_index("seq")]))
    block = own[:ROWS1]
    k1 = head_stack(first_view(block, mine), first_mask)
    v1 = head_stack(second_view(block, mine), second_mask)
    k1_part, v1_part = key_back(k1, v1, (qs[...],), (gs[...],))
    out[:, :FEAT] = level0[:, :FEAT] + scatter_rows(offsets, k1_part, None, 0)[:, :FEAT]
    out[:, FEAT:] = level0[:, FEAT:] + scatter_rows(offsets, v1_part, None, LANES - FEAT)[:, LANES - FEAT :]


def last_kernel(offsets, counts, own, all_qg, early, dk, dv):
    full = all_qg[...].reshape(GROUP * GROUP * ROWS2, PAIR + SIDE)
    helpers = full[:, PAIR:]
    queries, grads = first_view(full[:, :PAIR], helpers), second_view(full[:, :PAIR], helpers)
    mine = key_helpers(dilated_mask(offsets, 1, counts[lax.axis_index("seq")]))
    block = own[ROWS1:]
    k2 = head_stack(first_view(block, mine), first_mask)
    v2 = head_stack(second_view(block, mine), second_mask)
    k2_part, v2_part = key_back(k2, v2, (queries,), (grads,))
    dk[...] = to_paired((early[:, :FEAT] + scatter_rows(offsets, None, k2_part, 0)[:, :FEAT]) * SCALE)
    dv[...] = to_paired(early[:, FEAT:] + scatter_rows(offsets, None, v2_part, LANES - FEAT)[:, LANES - FEAT :])


def call(kernel, outs, n_smem, *args, scratch=()):
    return pl.pallas_call(
        kernel,
        out_shape=[jax.ShapeDtypeStruct(s, d) for s, d in outs],
        in_specs=[SMEM] * n_smem + [VMEM] * (len(args) - n_smem),
        out_specs=[VMEM] * len(outs),
        scratch_shapes=[pltpu.VMEM(s, BF) for s in scratch],
        compiler_params=pltpu.CompilerParams(vmem_limit_bytes=VMEM_BYTES),
    )(*args)


def first_call(offsets, keys, values):
    return pl.pallas_call(
        rows_kernel,
        out_shape=[jax.ShapeDtypeStruct(s, BF) for s in ((ROWS, PAIR), (GROUP, ROWS, PAIR))],
        in_specs=[pl.BlockSpec(memory_space=pl.ANY)] * 3,
        out_specs=[VMEM] * 2,
        scratch_shapes=[pltpu.SMEM(offsets.shape, offsets.dtype), pltpu.VMEM(keys.shape, BF), pltpu.VMEM(values.shape, BF)]
        + [pltpu.SemaphoreType.DMA(())] * 3,
        compiler_params=pltpu.CompilerParams(vmem_limit_bytes=60 * 1024 * 1024),
    )(offsets, keys, values)


def per_device(queries, keys, values, grad_y, out_weight, counts, offsets):
    n_seq = lax.axis_size("seq")
    rings = [[GROUP * b + i for i in range(GROUP)] for b in range(n_seq // GROUP)]
    planes = [[GROUP * b + i for b in range(n_seq // GROUP)] for i in range(GROUP)]

    def swap(x, bits):
        return lax.ppermute(x, "seq", [(i, i ^ bits) for i in range(n_seq)])

    def shift(x, step):
        return lax.ppermute(x, "seq", [(r[i], r[(i + step) % GROUP]) for r in rings for i in range(GROUP)])

    def exchange(copies, groups):
        return lax.all_to_all(copies, "seq", 0, 0, axis_index_groups=groups)

    def far(own, near):
        both = jnp.concatenate([own, near], axis=0)
        return tuple(shift(both, step) for step in (2, 4, 6))

    k_next, v_next = swap(keys, 1), swap(values, 1)
    own, copies = first_call(offsets, keys, values)
    copies, k_next, v_next = lax.optimization_barrier((copies, k_next, v_next))
    ring_kv = exchange(copies, rings)
    flat = (TOKENS, PAIR)
    kv, kvp = call(pairs_kernel, [(flat, BF)] * 2, 0, keys, values, k_next, v_next)
    gy = lax.all_gather(grad_y, "head", axis=0)
    qg, qg_top = call(
        proj_kernel, [((TOKENS + ROWS1, PAIR), BF), ((ROWS2, PAIR), BF)], 2, offsets, counts, gy, out_weight, queries
    )
    qgp = swap(qg, 1)
    (stats,) = call(level0_kernel, [((16, TOKENS), F32)], 1, counts, qg, kv, kvp)
    ring_kv, stats = lax.optimization_barrier((ring_kv, stats))
    (tail,) = call(
        level1_kernel, [((TAIL, PAIR), BF)], 2, offsets, counts, qg, qg_top, ring_kv, stats,
        scratch=[(2, GROUP * ROWS1, LANES)],
    )
    tail_next = swap(tail, 1)
    (repeated,) = call(repeat_kernel, [((GROUP, GROUP * ROWS2, PAIR), BF)], 0, ring_kv)
    repeated, tail_next, qgp = lax.optimization_barrier((repeated, tail_next, qgp))
    all_kv = exchange(repeated, planes)
    tails = far(tail[: 2 * ROWS2], tail_next[: 2 * ROWS2])
    tails, qgp = lax.optimization_barrier((jnp.concatenate([tail, tail_next, *tails], axis=0), qgp))
    big = (GROUP * GROUP * ROWS2, LANES)
    st_rows = 2 * TOKENS + GROUP * ROWS2
    st1, st, packed = call(
        finish_kernel, [((OWN, SIDE), BF), ((st_rows, SIDE), BF), ((GROUP, GROUP * ROWS2, PAIR + SIDE), BF)], 2, offsets, counts,
        tails, all_kv, scratch=[big, big],
    )
    near = jnp.concatenate([qg[TOKENS:], qgp[TOKENS:]], axis=0)
    qgs = tuple(shift(near, step) for step in (2, 4, 6))
    all_qg = exchange(packed, planes)
    (dq,) = call(
        grad_query_kernel, [((HALF, PAIR), BF)], 2, offsets, counts, qg, qg_top, st1, st, kv, kvp, ring_kv, all_kv,
        scratch=[(2, GROUP * ROWS1, LANES), big, big],
    )
    (level0,) = call(grad_key_kernel, [((TOKENS, PAIR), F32)], 1, counts, kv, qg, st, qgp)
    (early,) = call(
        level1_keys_kernel, [((TOKENS, PAIR), F32)], 2, offsets, counts, own, near, *qgs, st1, level0,
        scratch=[(OWN, LANES)] * 2,
    )
    dk, dv = call(last_kernel, [((HALF, PAIR), BF)] * 2, 2, offsets, counts, own, all_qg, early)
    return dq, dk, dv


def solution(mesh):
    split = P("seq", "head")
    return jax.shard_map(
        per_device,
        mesh=mesh,
        in_specs=(split, split, split, split, P("head", None), P(), P()),
        out_specs=(split, split, split),
        check_vma=False,
    )
```
